256 devices in a mesh: sector: 32 (over x, z), mpo: 8 (over y, core).
Axes of the slice: x: 4, y: 4, z: 8, core: 2. Of those that a mesh axis runs over, the one named last changes fastest.
Arguments:
- guess: float32 [64, 256, 256], P('sector'), may hold values from -17 to 17
- diagonal: float32 [64, 256, 256], P('sector'), may hold values from 0.5 to 5
- block_rows: int32 [64], P('sector'), may hold values from 128 to 256
- block_cols: int32 [64], P('sector'), may hold values from 128 to 256
- left_env: bfloat16 [40, 64, 256, 256], P('mpo', 'sector'), may hold values from -0.125 to 0.125
- right_env: bfloat16 [40, 64, 256, 256], P('mpo', 'sector'), may hold values from -0.375 to 0.375
- charge_shift: int32 [40], P('mpo'), may hold values from -1 to 1
- spin_shift: int32 [40], P('mpo'), may hold values from -1 to 1
Outputs:
- ground_state: float32 [64, 256, 256], P('sector', 'mpo')
- energy: float32 [], replicated
The draws below stay inside these ranges and needn't reach their ends.
All inputs are finite; a program needn't handle non-finite values.
Results may differ from the reference program's by a relative error of at most 0.011.
Values may be sent and summed in bfloat16 or wider, within the bound.
No kernel may reach another device: no remote copies, remote signals or barrier semaphores. Data moves between devices by JAX's collectives and lax.ppermute only.
A program may use at most 64 MiB of HBM per device.

```python
import math
import jax
import jax.numpy as jnp
from jax import lax

PB = 256
WMPO = 40
SEC_DEV = 2
ITERS = 4
CHARGES = 32
SECTORS = 64


def draw_guess(key, part):
    key = jax.random.fold_in(key, 11)
    key_values, key_rows, key_cols = jax.random.split(key, 3)
    array_shape = (SECTORS, PB, PB)
    values = jnp.clip(jax.random.normal(key_values, array_shape, jnp.float32), -5.0, 5.0)
    row_scale = 10.0 ** jax.random.uniform(key_rows, (SECTORS, PB, 1), jnp.float32)
    col_scale = 10.0 ** jax.random.uniform(key_cols, (SECTORS, 1, PB), jnp.float32)
    return values * jnp.sqrt(row_scale * col_scale) / 3.0


def plant(entries, stream_key, smallest, high):
    index_at = [jax.random.randint(jax.random.fold_in(stream_key, axis), (), 0, length) for axis, length in enumerate(entries.shape)]
    widest = entries.shape.index(max(entries.shape))
    neighbour = index_at[:widest] + [(index_at[widest] + 1) % entries.shape[widest]] + index_at[widest + 1:]
    return entries.at[tuple(index_at)].set(smallest).at[tuple(neighbour)].set(high)


def block_scale(rng, extent, pieces, least, top_value):
    def one(position, blocks):
        steps = jax.random.uniform(jax.random.fold_in(jax.random.fold_in(rng, 6), position), (blocks,), jnp.float32, least / len(pieces), top_value / len(pieces))
        return jnp.repeat(jnp.exp(steps), extent[position] // blocks).reshape((-1,) + (1,) * (len(extent) - position - 1))

    gain = one(*pieces[0])
    for cut in pieces[1:]:
        gain = gain * one(*cut)
    return gain


def bell_draw(own_key, shape, deviation, bound, pieces=(), kind=jnp.bfloat16):
    result = deviation * jax.random.normal(own_key, shape, jnp.float32)
    if pieces:
        result = result * block_scale(own_key, shape, pieces, -0.22, 0.18)
    return jnp.clip(result, -bound, bound).astype(kind)


def setup_inputs(seed: int = 0) -> dict:
    key_of = jax.random.split(jax.random.key(seed), 9)
    return {
        "guess": draw_guess(jax.random.fold_in(key_of[8], 71), 0),
        "diagonal": jnp.clip(jnp.exp(math.log(5.0) - 2.3025851 * jax.random.uniform(key_of[1], (SECTORS, PB, PB), jnp.float32) ** block_scale(key_of[1], (SECTORS, PB, PB), ((0, 32),), -0.2, 0.2)), 0.5, 5.0),
        "block_rows": plant(jax.random.randint(key_of[2], (SECTORS,), PB // 2, PB + 1), jax.random.fold_in(key_of[2], 1), PB // 2, PB).astype(jnp.int32),
        "block_cols": plant(jax.random.randint(key_of[3], (SECTORS,), PB // 2, PB + 1), jax.random.fold_in(key_of[3], 1), PB // 2, PB).astype(jnp.int32),
        "left_env": bell_draw(key_of[4], (WMPO, SECTORS, PB, PB), (8 * PB) ** -0.5, 0.125, ((0, 8), (1, 32))),
        "right_env": bell_draw(key_of[5], (WMPO, SECTORS, PB, PB), PB ** -0.5, 0.375, ((0, 8), (1, 32))),
        "charge_shift": plant(jax.random.randint(key_of[6], (WMPO,), -1, 2), jax.random.fold_in(key_of[6], 1), -1, 1).astype(jnp.int32),
        "spin_shift": plant(jax.random.randint(key_of[7], (WMPO,), -1, 2), jax.random.fold_in(key_of[7], 1), -1, 1).astype(jnp.int32),
    }


def move(field, charge_step, spin_step, direction):
    grid = field.reshape(CHARGES, SEC_DEV, PB, PB)
    padded = jnp.pad(grid, ((1, 1), (1, 1), (0, 0), (0, 0)))
    nought = jnp.zeros((), jnp.int32)
    corner = ((1 - direction * charge_step).astype(jnp.int32), (1 - direction * spin_step).astype(jnp.int32), nought, nought)
    return lax.dynamic_slice(padded, corner, (CHARGES, SEC_DEV, PB, PB)).reshape(SECTORS, PB, PB)

def live_mask(block_rows, block_cols):
    positions = jnp.arange(PB, dtype=jnp.int32)
    inside = (positions[None, :, None] < block_rows[:, None, None]) & (positions[None, None, :] < block_cols[:, None, None])
    return inside.astype(jnp.float32)

def apply_operator(vector, left_env, right_env, charge_shift, spin_shift, diagonal, live):
    vector_f = vector.astype(jnp.bfloat16).astype(jnp.float32)

    def one_index(total, items):
        left_block, right_block, charge_step, spin_step = items
        left_f = left_block.astype(jnp.float32)
        right_f = right_block.astype(jnp.float32)
        source = move(vector_f, charge_step, spin_step, 1)
        middle = jnp.einsum('sij,sjl->sil', left_f, source).astype(jnp.bfloat16)
        middle = lax.optimization_barrier(middle).astype(jnp.float32)
        forward = jnp.einsum('sil,sml->sim', middle, right_f)
        back = jnp.einsum('sji,sjl->sil', left_f, vector_f).astype(jnp.bfloat16)
        back = lax.optimization_barrier(back).astype(jnp.float32)
        turned = jnp.einsum('sil,slm->sim', back, right_f)
        return (total + forward + move(turned, charge_step, spin_step, -1), None)
    total, unused_out = lax.scan(one_index, jnp.zeros(vector.shape, jnp.float32), (left_env, right_env, charge_shift, spin_shift))
    return live * (total + diagonal * vector)

def reference(guess, diagonal, block_rows, block_cols, left_env, right_env, charge_shift, spin_shift):
    total_norm = float(SECTORS * PB * PB)
    live = live_mask(block_rows, block_cols)

    def operate(vector):
        return apply_operator(vector, left_env, right_env, charge_shift, spin_shift, diagonal, live)
    vector = live * guess
    start_norm = jnp.sum(vector * vector) / total_norm
    vector = vector / jnp.sqrt(start_norm + 1e-06)
    image = operate(vector)
    rayleigh = jnp.sum(vector * image) / total_norm
    for iteration in range(ITERS):
        residual = image - rayleigh * vector
        precond = residual / diagonal
        correlation = jnp.sum(vector * precond) / total_norm
        correction = precond - correlation * vector
        length_sq = jnp.sum(correction * correction) / total_norm
        correction = correction / jnp.sqrt(length_sq + 1e-06)
        turned_image = operate(correction)
        off_diag = jnp.sum(vector * turned_image) / total_norm
        corr_energy = jnp.sum(correction * turned_image) / total_norm
        half_gap = 0.5 * (corr_energy - rayleigh)
        lowest = 0.5 * (rayleigh + corr_energy) - jnp.sqrt(half_gap * half_gap + off_diag * off_diag)
        weight_old = corr_energy - lowest
        length_pair = jnp.sqrt(weight_old * weight_old + off_diag * off_diag)
        keep_share = weight_old / length_pair
        mix_share = -off_diag / length_pair
        vector = keep_share * vector + mix_share * correction
        image = keep_share * image + mix_share * turned_image
        rayleigh = lowest
    return (vector, rayleigh)
```

```python
import functools

import jax
import jax.numpy as jnp
from jax import lax
from jax.experimental import pallas as pl
from jax.experimental.pallas import tpu as pltpu
from jax.sharding import Mesh
from jax.sharding import PartitionSpec as P

ITERS = 4
BLOCK = 256
HALF = BLOCK // 2
SPINS = 2
CELLS = 3 * SPINS
CHUNK = 32
SECTOR = ("x", "z")
SUMMED = ("x", "z", "core")
BF16 = jnp.bfloat16
F32 = jnp.float32
VMEM_LIMIT = 40 * 1024 * 1024

CORE, ROWS, COLS, CELL_AT = 0, 1, 3, 5


def pair_sum(product):
    total = product[:8]
    for start in range(8, product.shape[0], 8):
        total = total + product[start : start + 8]
    return total[:, :128] + total[:, 128:]


def mask_of(info, spin, row_start, rows):
    row = lax.broadcasted_iota(jnp.int32, (rows, BLOCK), 0) + row_start
    col = lax.broadcasted_iota(jnp.int32, (rows, BLOCK), 1)
    return (row < info[ROWS + spin]) & (col < info[COLS + spin])


def pick(sums, index):
    lane = lax.broadcasted_iota(jnp.int32, sums.shape, 1)
    return jnp.sum(jnp.where(lane == index, sums, 0.0), axis=1, keepdims=True)


def pair_products(info, vector_b, left, right, total):
    total[...] = jnp.zeros_like(total)
    for spin in range(SPINS):
        own = vector_b[SPINS + spin]
        for w in range(left.shape[0]):
            cell = info[CELL_AT + w * SPINS + spin]
            lw = left[w, spin]
            rw = right[w, spin]
            middle = jnp.dot(lw, vector_b[cell], preferred_element_type=F32).astype(BF16)
            back = lax.dot_general(
                lw, own, (((0,), (0,)), ((), ())), preferred_element_type=F32
            ).astype(BF16)
            total[SPINS + spin] += lax.dot_general(
                middle, rw, (((1,), (1,)), ((), ())), preferred_element_type=F32
            )
            total[cell] += jnp.dot(back, rw, preferred_element_type=F32)


def hand_out(info, total, keep, send):
    core = info[CORE]
    mine = pl.ds(pl.multiple_of(core * HALF, HALF), HALF)
    other = pl.ds(pl.multiple_of((1 - core) * HALF, HALF), HALF)
    for cell in range(CELLS):
        keep[cell] = total[cell, mine, :]
        send[cell] = total[cell, other, :].astype(BF16)


def start_kernel(
    info, guess, one_a, two_a, one_b, two_b, left, right, vector, keep, send, vector_b, total
):
    core = info[CORE]
    for spin in range(SPINS):
        for start in range(0, BLOCK, HALF):
            inside = mask_of(info, spin, start, HALF)
            value = jnp.where(inside, guess[spin, start : start + HALF], 0.0)
            vector[SPINS + spin, start : start + HALF] = value
            vector_b[SPINS + spin, start : start + HALF] = value.astype(BF16)
    for slot, piece, place in (
        (0, one_a, core), (2, two_a, core), (0, one_b, 1 - core), (2, two_b, 1 - core)
    ):
        rows = pl.ds(pl.multiple_of(place * HALF, HALF), HALF)
        for spin in range(SPINS):
            value = piece[spin]
            vector[slot * SPINS + spin, rows, :] = value
            vector_b[slot * SPINS + spin, rows, :] = value.astype(BF16)
    vector_b[CELLS] = jnp.zeros((BLOCK, BLOCK), BF16)
    pair_products(info, vector_b, left, right, total)
    hand_out(info, total, keep, send)


def sums_kernel(first, last, info, part, turn_one, turn_two, turn_three, diagonal, *rest):
    if first:
        correction, image, sums = rest
    else:
        vector, residual, correction, rayleigh, image, sums = rest
        old = rayleigh[0:1, 0:1]
    core = info[CORE]
    names = None
    step = 16
    count = 22

    def one(spin, index, totals):
        start = pl.multiple_of(index * step, step)
        rows = pl.ds(start, step)
        c = correction[spin, rows, :]
        d = diagonal[spin, rows, :]
        summed = (part[spin, rows, :].astype(F32) + turn_two[spin, rows, :].astype(F32)) + (
            turn_one[spin, rows, :].astype(F32) + turn_three[spin, rows, :].astype(F32)
        )
        inside = mask_of(info, spin, core * HALF + start, step)
        hc_b = jnp.where(inside, summed + d * c, 0.0).astype(BF16)
        hc = hc_b.astype(F32)
        if not last:
            image[spin, rows, :] = hc_b
        pairs = {}
        if not first:
            x = vector[spin, rows, :]
            pairs[0] = (x, hc)
        pairs[1] = (c, hc)
        if not last:
            pairs[4] = (c, c)
            inv = 1.0 / d
            cd = c * inv
            pairs[11] = (c, cd)
            pairs[21] = (cd, cd)
            if first:
                g = hc
            else:
                g = hc - old * c
            gd = g * inv
            pairs[8] = (c, gd)
            pairs[14] = (gd, gd)
            pairs[18] = (gd, cd)
            if not first:
                res = residual[spin, rows, :]
                rd = res * inv
                xd = x * inv
                pairs[2] = (x, x)
                pairs[3] = (x, c)
                pairs[5] = (x, rd)
                pairs[6] = (x, gd)
                pairs[7] = (c, rd)
                pairs[9] = (x, xd)
                pairs[10] = (x, cd)
                pairs[12] = (rd, rd)
                pairs[13] = (rd, gd)
                pairs[15] = (rd, xd)
                pairs[16] = (rd, cd)
                pairs[17] = (gd, xd)
                pairs[19] = (xd, xd)
                pairs[20] = (xd, cd)
        return tuple(
            total + pair_sum(pairs[at][0] * pairs[at][1]) if at in pairs else total
            for at, total in enumerate(totals)
        )

    totals = tuple(jnp.zeros((8, 128), F32) for _ in range(count))
    for spin in range(SPINS):
        totals = lax.fori_loop(0, HALF // step, functools.partial(one, spin), totals)
    lane = lax.broadcasted_iota(jnp.int32, (1, 128), 1)
    row = jnp.zeros((1, 128), F32)
    for at, total in enumerate(totals):
        value = jnp.sum(jnp.sum(total, axis=0, keepdims=True), axis=1, keepdims=True)
        row = row + jnp.where(lane == at, value, 0.0)
    sums[...] = jnp.broadcast_to(row[None], sums.shape)


def rotation(totals, norm, rayleigh):
    off_diag = totals(0)
    corr_energy = totals(1)
    half_gap = 0.5 * (corr_energy - rayleigh)
    lowest = 0.5 * (rayleigh + corr_energy) - jnp.sqrt(half_gap * half_gap + off_diag * off_diag)
    weight_old = corr_energy - lowest
    length_pair = jnp.sqrt(weight_old * weight_old + off_diag * off_diag)
    return weight_old / length_pair, -off_diag / length_pair, lowest


def step_kernel(first, norm, info, gathered, *rest):
    if first:
        (diag, done_a, dtwo_a, done_b, dtwo_b, hzero_a, hone_a, htwo_a, hzero_b, hone_b, htwo_b,
         c_in, left, right, x_out, res_out, c_out, inv_out, ray_out, keep, send,
         vector_b, total) = rest
    else:
        (hzero_a, hone_a, htwo_a, hzero_b, hone_b, htwo_b, x_in, res_in, c_in, inv_in, ray_in,
         left, right, x_out, res_out, c_out, ray_out, keep, send, vector_b, total) = rest
    core = info[CORE]
    sums = jnp.sum(gathered[...], axis=0) * (1.0 / norm)

    def t(at):
        return pick(sums, at)

    cc, b7, d10, b4, d3, d7 = t(4), t(11), t(21), t(8), t(14), t(18)
    if first:
        scale = lax.rsqrt(cc + 1e-06)
        m = scale
        new = t(1) * scale * scale
        shift = -new
        mm = m * m
        corr = mm * (b4 + shift * b7)
        pp = mm * (d3 + 2.0 * shift * d7 + shift * shift * d10)
        xx = mm * cc
        old = None
    else:
        old = ray_in[0:1, 0:1]
        k, m, new = rotation(t, norm, old)
        shift = old - new
        kk, km, mm = k * k, k * m, m * m
        corr = (kk * t(5) + km * (t(6) + t(7)) + mm * b4) + shift * (
            kk * t(9) + 2.0 * km * t(10) + mm * b7
        )
        pp = (
            (kk * t(12) + 2.0 * km * t(13) + mm * d3)
            + 2.0 * shift * (kk * t(15) + km * (t(16) + t(17)) + mm * d7)
            + shift * shift * (kk * t(19) + 2.0 * km * t(20) + mm * d10)
        )
        xx = kk * t(2) + 2.0 * km * t(3) + mm * cc
    length_sq = jnp.maximum(pp - corr * corr * (2.0 - xx), 0.0)
    inv_length = lax.rsqrt(length_sq + 1e-06)
    ray_out[...] = jnp.broadcast_to(new, ray_out.shape)

    for slot, half, piece in (
        (0, 0, hone_a), (1, 0, hzero_a), (2, 0, htwo_a),
        (0, 1, hone_b), (1, 1, hzero_b), (2, 1, htwo_b),
    ):
        place = core if half == 0 else 1 - core
        for spin in range(SPINS):
            cell = slot * SPINS + spin

            def one(index, carry, cell=cell, spin=spin, slot=slot, half=half, place=place,
                    piece=piece):
                start = pl.multiple_of(index * CHUNK, CHUNK)
                there = pl.ds(start, CHUNK)
                rows = pl.ds(pl.multiple_of(place * HALF + start, CHUNK), CHUNK)
                hc = piece[spin, there, :].astype(F32)
                c = c_in[cell, rows, :]
                if first:
                    if slot == 1:
                        d = diag[spin, rows, :]
                    else:
                        source = {0: (done_a, done_b), 2: (dtwo_a, dtwo_b)}[slot][half]
                        d = source[spin, there, :]
                    inv = jnp.where(d > 0.0, 1.0 / jnp.where(d > 0.0, d, 1.0), 0.0)
                    inv_out[cell, rows, :] = inv
                    x = m * c
                    res = m * hc + shift * x
                else:
                    inv = inv_in[cell, rows, :]
                    x = k * x_in[cell, rows, :] + m * c
                    res = k * res_in[cell, rows, :] + m * (hc - old * c) + shift * x
                new_c = (res * inv - corr * x) * inv_length
                x_out[cell, rows, :] = x
                res_out[cell, rows, :] = res
                c_out[cell, rows, :] = new_c
                vector_b[cell, rows, :] = new_c.astype(BF16)
                return carry

            lax.fori_loop(0, HALF // CHUNK, one, 0)
    vector_b[CELLS] = jnp.zeros((BLOCK, BLOCK), BF16)
    pair_products(info, vector_b, left, right, total)
    hand_out(info, total, keep, send)


def end_kernel(norm, gathered, ray_in, x_in, c_in, out, energy):
    sums = jnp.sum(gathered[...], axis=0) * (1.0 / norm)
    k, m, new = rotation(lambda at: pick(sums, at), norm, ray_in[0:1, 0:1])
    out[...] = k * x_in[...] + m * c_in[...]
    energy[...] = jnp.broadcast_to(new, energy.shape)


def whole(count):
    return [pl.BlockSpec(memory_space=pltpu.VMEM)] * count


def shape(dims, dtype):
    return jax.ShapeDtypeStruct(dims, dtype)


STATE = (CELLS, BLOCK, BLOCK)
PIECE = (SPINS, HALF, BLOCK)
SIDE = (CELLS, HALF, BLOCK)


def params():
    return pltpu.CompilerParams(vmem_limit_bytes=VMEM_LIMIT)


def call_vmem(kernel, info, outs, scratch, *args):
    return pl.pallas_call(
        kernel,
        in_specs=[pl.BlockSpec(memory_space=pltpu.SMEM)] + whole(len(args)),
        out_specs=whole(len(outs)),
        out_shape=outs,
        scratch_shapes=scratch,
        compiler_params=params(),
    )(info, *args)


def product_scratch():
    return [pltpu.VMEM((CELLS + 1, BLOCK, BLOCK), BF16), pltpu.VMEM((CELLS + 1, BLOCK, BLOCK), F32)]


def call_sums(first, last, peers, info, part, turns, diagonal, state, rayleigh):
    def piece(index, info):
        return (0, 0, 0)

    def own(index, info):
        return (1, info[CORE], 0)

    def own_diag(index, info):
        return (0, info[CORE], 0)

    specs = [pl.BlockSpec(PIECE, piece)] * 4 + [pl.BlockSpec(PIECE, own_diag)]
    specs += [pl.BlockSpec(PIECE, own)] * len(state)
    args = [part, *turns, diagonal, *state]
    if not first:
        specs.append(pl.BlockSpec((8, 128), lambda index, info: (0, 0)))
        args.append(rayleigh)
    return pl.pallas_call(
        functools.partial(sums_kernel, first, last),
        grid_spec=pltpu.PrefetchScalarGridSpec(
            num_scalar_prefetch=1,
            grid=(1,),
            in_specs=specs,
            out_specs=[
                pl.BlockSpec(PIECE, piece),
                pl.BlockSpec((peers, 1, 128), piece),
            ],
        ),
        out_shape=[shape(PIECE, BF16), shape((peers, 1, 128), F32)],
        compiler_params=params(),
    )(info, *args)


def on_device(
    guess, diagonal, block_rows, block_cols, left_env, right_env, charge_shift, spin_shift
):
    sectors = lax.axis_size("x") * lax.axis_size("z")
    norm = float(sectors * SPINS * BLOCK * BLOCK)
    pair_one = [(i, i ^ 1) for i in range(sectors)]
    pair_two = [(i, j) for i in range(sectors) for j in (((i + 1) ^ 1) - 1,) if 0 <= j < sectors]
    core_pair = [(0, 1), (1, 0)]
    y_size = lax.axis_size("y")
    peers = sectors * lax.axis_size("core")

    core = lax.axis_index("core")
    sector = lax.axis_index(SECTOR)
    side = 1 - 2 * (sector % 2)
    spins = jnp.arange(SPINS, dtype=jnp.int32)
    source = spins[None, :] - spin_shift[:, None]
    cell = (1 + side * charge_shift[:, None]) * SPINS + source
    cell = jnp.where((source >= 0) & (source < SPINS), cell, CELLS)
    info = jnp.concatenate(
        [jnp.reshape(core, (1,)), block_rows, block_cols, jnp.reshape(cell, (-1,))]
    ).astype(jnp.int32)

    def with_partners(own):
        return (
            lax.ppermute(own, SECTOR, pair_one),
            lax.ppermute(own, SECTOR, pair_two),
        )

    def other_core(value):
        return lax.ppermute(value, "core", core_pair)

    def own_half(value):
        return lax.dynamic_slice_in_dim(value, core * HALF, HALF, 1)

    def reduced(keep, send):
        both = keep + other_core(send).astype(F32)
        to_one = both[:SPINS].astype(BF16)
        to_two = both[2 * SPINS :].astype(BF16)
        from_one = lax.ppermute(to_one, SECTOR, pair_one)
        from_two = lax.ppermute(to_two, SECTOR, pair_two)
        part = (both[SPINS : 2 * SPINS] + from_one.astype(F32) + from_two.astype(F32)).astype(BF16)
        turns = [
            lax.ppermute(part, "y", [(i, (i + turn) % y_size) for i in range(y_size)])
            for turn in (1, 2, 3)
        ]
        return part, turns

    def spread(image, sums):
        one_a, two_a = with_partners(image)
        zero_b = other_core(image)
        gathered = lax.all_to_all(sums, SUMMED, 0, 0, tiled=True)
        return gathered, (image, one_a, two_a, zero_b, other_core(one_a), other_core(two_a))

    positions = jnp.arange(BLOCK, dtype=jnp.int32)
    inside = (positions[None, :, None] < block_rows[:, None, None]) & (
        positions[None, None, :] < block_cols[:, None, None]
    )
    masked = own_half(jnp.where(inside, guess, 0.0))
    one_a, two_a = with_partners(masked)
    correction, keep, send = call_vmem(
        start_kernel, info,
        [shape(STATE, F32), shape(SIDE, F32), shape(SIDE, BF16)], product_scratch(),
        guess, one_a, two_a, other_core(one_a), other_core(two_a), left_env, right_env,
    )
    done_a, dtwo_a = with_partners(own_half(diagonal))
    diags = (diagonal, done_a, dtwo_a, other_core(done_a), other_core(dtwo_a))
    part, turns = reduced(keep, send)
    image, sums = call_sums(True, False, peers, info, part, turns, diagonal, (correction,), None)
    outs = [shape(STATE, F32)] * 3
    tail = [shape((8, 128), F32), shape(SIDE, F32), shape(SIDE, BF16)]
    for iteration in range(ITERS):
        gathered, pieces = spread(image, sums)
        if iteration == 0:
            vector, residual, correction, inverse, rayleigh, keep, send = call_vmem(
                functools.partial(step_kernel, True, norm), info,
                outs + [shape(STATE, F32)] + tail, product_scratch(),
                gathered, *diags, *pieces, correction, left_env, right_env,
            )
        else:
            vector, residual, correction, rayleigh, keep, send = call_vmem(
                functools.partial(step_kernel, False, norm), info,
                outs + tail, product_scratch(),
                gathered, *pieces, vector, residual, correction, inverse, rayleigh,
                left_env, right_env,
            )
        part, turns = reduced(keep, send)
        last = iteration == ITERS - 1
        image, sums = call_sums(
            False, last, peers, info, part, turns, diagonal,
            (vector, residual, correction), rayleigh,
        )
    gathered = lax.all_to_all(sums, SUMMED, 0, 0, tiled=True)
    share = BLOCK // (y_size * lax.axis_size("core"))
    at = (lax.axis_index("y") * lax.axis_size("core") + core) * share

    def slice_of(value):
        return lax.dynamic_slice(value, (SPINS, at, 0), (SPINS, share, BLOCK))

    ground_state, energy = pl.pallas_call(
        functools.partial(end_kernel, norm),
        in_specs=whole(4),
        out_specs=whole(2),
        out_shape=[shape((SPINS, share, BLOCK), F32), shape((8, 128), F32)],
    )(gathered, rayleigh, slice_of(vector), slice_of(correction))
    return ground_state, energy[0, 0]


def solution(mesh):
    fine = Mesh(mesh.devices.reshape(4, 8, 4, 2), ("x", "z", "y", "core"))
    mpo = ("y", "core")
    return jax.shard_map(
        on_device,
        mesh=fine,
        in_specs=(
            P(SECTOR, None, None),
            P(SECTOR, None, None),
            P(SECTOR),
            P(SECTOR),
            P(mpo, SECTOR, None, None),
            P(mpo, SECTOR, None, None),
            P(mpo),
            P(mpo),
        ),
        out_specs=(P(SECTOR, mpo, None), P()),
        check_vma=False,
    )
```

```python
import functools

import jax
import jax.numpy as jnp
from jax import lax
from jax.experimental import pallas as pl
from jax.experimental.pallas import tpu as pltpu
from jax.sharding import Mesh
from jax.sharding import PartitionSpec as P

ITERS = 4
BLOCK = 256
HALF = BLOCK // 2
SHARE = 32
SHARES = HALF // SHARE
SPINS = 2
CELLS = 3 * SPINS
AHEAD = CELLS + 1
SUMS = 6
SECTOR = ("x", "z")
EVERYONE = ("x", "z", "y", "core")
HALVES = ("x", "z", "core")
BF16 = jnp.bfloat16
F32 = jnp.float32
VMEM_LIMIT = 24 * 1024 * 1024

HALF_BLOCK = (SPINS, HALF, BLOCK)
SIDE = (CELLS, HALF, BLOCK)


def block_rows_of(share, core):
    return pl.ds(pl.multiple_of((2 * share + core) * SHARE, SHARE), SHARE)


def half_rows_of(share):
    return pl.ds(pl.multiple_of(share * SHARE, SHARE), SHARE)


def inside_of(rows, cols, spin, first_row, count):
    row = lax.broadcasted_iota(jnp.int32, (count, BLOCK), 0) + first_row
    col = lax.broadcasted_iota(jnp.int32, (count, BLOCK), 1)
    return (row < rows[spin]) & (col < cols[spin])


def pair_sum(product):
    total = product[:8]
    for start in range(8, product.shape[0], 8):
        total = total + product[start : start + 8]
    return total[:, :128] + total[:, 128:]


def pick(sums, index):
    lane = lax.broadcasted_iota(jnp.int32, sums.shape, 1)
    return jnp.sum(jnp.where(lane == index, sums, 0.0), axis=1, keepdims=True)


def reduced(totals):
    lane = lax.broadcasted_iota(jnp.int32, (1, 128), 1)
    row = jnp.zeros((1, 128), F32)
    for at, total in enumerate(totals):
        value = jnp.sum(jnp.sum(total, axis=0, keepdims=True), axis=1, keepdims=True)
        row = row + jnp.where(lane == at, value, 0.0)
    return row


def zeros(count):
    return tuple(jnp.zeros((8, 128), F32) for _ in range(count))


def guess_kernel(rows, cols, guess, vector, vector_b):
    core = lax.axis_index("core")
    for spin in range(SPINS):
        for share in range(SHARES):
            there = block_rows_of(share, core)
            here = half_rows_of(share)
            inside = inside_of(rows, cols, spin, (2 * share + core) * SHARE, SHARE)
            value = jnp.where(inside, guess[spin, there, :], 0.0)
            vector[spin, here, :] = value
            vector_b[spin, here, :] = value.astype(BF16)


def diagonal_kernel(rows, cols, diagonal, vector, diag, inverse, sums):
    core = lax.axis_index("core")
    totals = zeros(SUMS)
    for spin in range(SPINS):
        for share in range(SHARES):
            here = half_rows_of(share)
            inside = inside_of(rows, cols, spin, (2 * share + core) * SHARE, SHARE)
            d = diagonal[spin, block_rows_of(share, core), :]
            diag[spin, here, :] = d
            inverse[spin, here, :] = jnp.where(inside, 1.0 / d, 0.0)
            value = vector[spin, here, :]
            totals = totals[:1] + (totals[1] + pair_sum(value * value),) + totals[2:5] + (
                totals[5] + pair_sum(value * value * d),
            )
    sums[...] = jnp.broadcast_to(reduced(totals), sums.shape)


def products_kernel(
    last, copies, shifts, zero_a, low_a, high_a, zero_b, low_b, high_b, left, right, *rest
):
    if last:
        state_sums, sums, vector_b, total = rest
    else:
        keep, send, vector_b, total = rest
    core = lax.axis_index("core")
    charges = lax.axis_size("x") * lax.axis_size("z")
    own_charge = lax.axis_index("x") * lax.axis_size("z") + lax.axis_index("z")
    indices = left.shape[0]
    for slot, piece, half in (
        (1, zero_a, core), (1, zero_b, 1 - core), (0, low_a, core), (0, low_b, 1 - core),
        (2, high_a, core), (2, high_b, 1 - core),
    ):
        for spin in range(SPINS):
            for share in range(SHARES):
                vector_b[slot * SPINS + spin, block_rows_of(share, half), :] = piece[
                    spin, half_rows_of(share), :
                ]
    vector_b[CELLS] = jnp.zeros((BLOCK, BLOCK), BF16)
    total[...] = jnp.zeros_like(total)
    for spin in range(SPINS):
        own = vector_b[SPINS + spin]
        for w in range(indices):
            charge = shifts[w]
            there = own_charge - charge
            source = spin - shifts[indices + w]
            on_grid = (source >= 0) & (source < SPINS) & (there >= 0) & (there < charges)
            cell = jnp.where(on_grid, (1 - charge) * SPINS + source, CELLS)
            lw = left[w, spin]
            rw = right[w, spin]
            middle = jnp.dot(lw, vector_b[cell], preferred_element_type=F32).astype(BF16)
            back = lax.dot_general(
                lw, own, (((0,), (0,)), ((), ())), preferred_element_type=F32
            ).astype(BF16)
            total[AHEAD + spin if last else SPINS + spin] += lax.dot_general(
                middle, rw, (((1,), (1,)), ((), ())), preferred_element_type=F32
            )
            total[cell] += jnp.dot(back, rw, preferred_element_type=F32)
    if not last:
        for cell in range(CELLS):
            for share in range(SHARES):
                here = half_rows_of(share)
                keep[cell, here, :] = total[cell, block_rows_of(share, core), :]
                send[cell, here, :] = total[cell, block_rows_of(share, 1 - core), :].astype(BF16)
        return
    energy = jnp.zeros((8, 128), F32)
    for spin in range(SPINS):

        def one(index, energy, spin=spin):
            there = pl.ds(pl.multiple_of(index * SHARE, SHARE), SHARE)
            vector = vector_b[SPINS + spin, there, :].astype(F32)
            return energy + pair_sum(total[AHEAD + spin, there, :] * vector)

        energy = lax.fori_loop(0, BLOCK // SHARE, one, energy, unroll=True)
    row = reduced(zeros(SUMS - 1) + (2.0 * energy,)) + state_sums[0:1, :] * (1.0 / copies)
    sums[...] = jnp.broadcast_to(row, sums.shape)


def image_rows(spin, here, part, turn_one, turn_two, turn_three):
    return (part[spin, here, :].astype(F32) + turn_two[spin, here, :].astype(F32)) + (
        turn_one[spin, here, :].astype(F32) + turn_three[spin, here, :].astype(F32)
    )


def energy_kernel(part, turn_one, turn_two, turn_three, p, state_sums, sums):
    energy = zeros(1)[0]
    for spin in range(SPINS):

        def one(index, energy, spin=spin):
            here = half_rows_of(index)
            image = image_rows(spin, here, part, turn_one, turn_two, turn_three)
            return energy + pair_sum(image * p[spin, here, :])

        energy = lax.fori_loop(0, SHARES, one, energy, unroll=True)
    row = reduced(zeros(SUMS - 1) + (energy,)) + state_sums[0:1, :]
    sums[...] = jnp.broadcast_to(row, sums.shape)


def rotation(t, rayleigh):
    corr = t(0)
    image_p = t(3) + rayleigh * corr
    image_x = t(4) + rayleigh * t(2)
    length_sq = jnp.maximum(t(1) - corr * corr * (2.0 - t(2)), 0.0)
    inv_length = lax.rsqrt(length_sq + 1e-06)
    off_diag = (image_p - corr * image_x) * inv_length
    corr_energy = (t(5) - 2.0 * corr * image_p + corr * corr * image_x) * inv_length * inv_length
    half_gap = 0.5 * (corr_energy - rayleigh)
    lowest = 0.5 * (rayleigh + corr_energy) - jnp.sqrt(half_gap * half_gap + off_diag * off_diag)
    weight_old = corr_energy - lowest
    length_pair = jnp.sqrt(weight_old * weight_old + off_diag * off_diag)
    mix = -off_diag / length_pair * inv_length
    return weight_old / length_pair - mix * corr, mix, lowest


def step_kernel(first, norm, gathered, part, turn_one, turn_two, turn_three, *rest):
    if first:
        (diag, inverse, p_in, x_out, res_out, p_out, p_b, ray_out, sums_out) = rest
    else:
        (diag, inverse, x_in, res_in, p_in, ray_in,
         x_out, res_out, p_out, p_b, ray_out, sums_out) = rest
    sums = jnp.sum(gathered[...], axis=0, keepdims=True) * (1.0 / norm)

    def t(at):
        return pick(sums, at)

    if first:
        m = lax.rsqrt(t(1) + 1e-06)
        new = t(5) * m * m
        shift = -new
    else:
        old = ray_in[0:1, 0:1]
        a, m, new = rotation(t, old)
        shift = old - new
    ray_out[...] = jnp.broadcast_to(new, ray_out.shape)
    step = 16

    def one(spin, index, totals):
        here = pl.ds(pl.multiple_of(index * step, step), step)
        summed = image_rows(spin, here, part, turn_one, turn_two, turn_three)
        d = diag[spin, here, :]
        p = p_in[spin, here, :]
        image = summed + d * p
        if first:
            x = m * p
            res = m * image + shift * x
        else:
            x = a * x_in[spin, here, :] + m * p
            res = a * res_in[spin, here, :] + m * (image - old * p) + shift * x
        new_p = res * inverse[spin, here, :]
        x_out[spin, here, :] = x
        res_out[spin, here, :] = res
        p_out[spin, here, :] = new_p
        p_b[spin, here, :] = new_p.astype(BF16)
        pairs = ((x, new_p), (new_p, new_p), (x, x), (res, new_p), (res, x), (new_p * d, new_p))
        return tuple(total + pair_sum(u * v) for total, (u, v) in zip(totals, pairs))

    totals = zeros(SUMS)
    for spin in range(SPINS):
        totals = lax.fori_loop(0, HALF // step, functools.partial(one, spin), totals)
    sums_out[...] = jnp.broadcast_to(reduced(totals), sums_out.shape)


def end_kernel(norm, gathered, ray_in, x_in, p_in, out, energy):
    sums = jnp.sum(gathered[...], axis=0, keepdims=True) * (1.0 / norm)
    a, m, new = rotation(lambda at: pick(sums, at), ray_in[0:1, 0:1])
    here = half_rows_of(lax.axis_index("y"))
    for spin in range(SPINS):
        out[spin] = a * x_in[spin, here, :] + m * p_in[spin, here, :]
    energy[0, 0] = new[0, 0]


def shape(dims, dtype):
    return jax.ShapeDtypeStruct(dims, dtype)


def call(kernel, scalars, arrays, outs, scratch=(), out_specs=None):
    vmem = pl.BlockSpec(memory_space=pltpu.VMEM)
    return pl.pallas_call(
        kernel,
        in_specs=[pl.BlockSpec(memory_space=pltpu.SMEM)] * len(scalars) + [vmem] * len(arrays),
        out_specs=out_specs or [vmem] * len(outs),
        out_shape=outs,
        scratch_shapes=scratch,
        compiler_params=pltpu.CompilerParams(vmem_limit_bytes=VMEM_LIMIT),
    )(*scalars, *arrays)


def on_device(
    guess, diagonal, block_rows, block_cols, left_env, right_env, charge_shift, spin_shift
):
    sectors = lax.axis_size("x") * lax.axis_size("z")
    y_size = lax.axis_size("y")
    peers = sectors * lax.axis_size("core")
    everyone = peers * y_size
    norm = float(sectors * SPINS * BLOCK * BLOCK)
    upward = [(i, (i + 1) % sectors) for i in range(sectors)]
    downward = [(j, i) for i, j in upward]
    core_pair = [(0, 1), (1, 0)]
    shifts = jnp.concatenate([charge_shift, spin_shift])

    def other_core(value):
        return lax.ppermute(value, "core", core_pair)

    def products(p_b, state_sums=None):
        last = state_sums is not None
        low_a = lax.ppermute(p_b, SECTOR, upward)
        high_a = lax.ppermute(p_b, SECTOR, downward)
        pieces = [p_b, low_a, high_a, other_core(p_b), other_core(low_a), other_core(high_a)]
        cells = AHEAD + SPINS if last else CELLS + 1
        return call(
            functools.partial(products_kernel, last, y_size), [shifts],
            [*pieces, left_env, right_env] + ([state_sums] if last else []),
            [shape((everyone, 128), F32)] if last else [shape(SIDE, F32), shape(SIDE, BF16)],
            [pltpu.VMEM((CELLS + 1, BLOCK, BLOCK), BF16), pltpu.VMEM((cells, BLOCK, BLOCK), F32)],
        )

    def image_parts(keep, send):
        both = keep + other_core(send).astype(F32)
        from_high = lax.ppermute(both[:SPINS].astype(BF16), SECTOR, downward)
        from_low = lax.ppermute(both[2 * SPINS :].astype(BF16), SECTOR, upward)
        part = both[SPINS : 2 * SPINS] + from_high.astype(F32) + from_low.astype(F32)
        part = part.astype(BF16)
        turns = [
            lax.ppermute(part, "y", [(i, (i + turn) % y_size) for i in range(y_size)])
            for turn in (1, 2, 3)
        ]
        return [part, *turns]

    state = shape(HALF_BLOCK, F32)
    state_b = shape(HALF_BLOCK, BF16)
    flat = shape((8, 128), F32)
    masks = [block_rows, block_cols]
    p, p_b = call(guess_kernel, masks, [guess], [state, state_b])
    diag, inverse, state_sums = call(
        diagonal_kernel, masks, [diagonal, p], [state, state, flat]
    )
    before = [p]
    for iteration in range(ITERS):
        parts = image_parts(*products(p_b))
        sums = call(energy_kernel, [], [*parts, p, state_sums], [shape((peers, 128), F32)])[0]
        gathered = lax.all_to_all(sums, HALVES, 0, 0, tiled=True)
        vector, residual, p, p_b, rayleigh, state_sums = call(
            functools.partial(step_kernel, iteration == 0, norm), [],
            [gathered, *parts, diag, inverse, *before],
            [state] * 3 + [state_b, flat, flat],
        )
        before = [vector, residual, p, rayleigh]
    gathered = lax.all_to_all(products(p_b, state_sums)[0], EVERYONE, 0, 0, tiled=True)
    vmem = pl.BlockSpec(memory_space=pltpu.VMEM)
    ground_state, energy = call(
        functools.partial(end_kernel, norm), [], [gathered, rayleigh, vector, p],
        [shape((SPINS, SHARE, BLOCK), F32), shape((1, 1), F32)],
        out_specs=[vmem, pl.BlockSpec(memory_space=pltpu.SMEM)],
    )
    return ground_state, energy[0, 0]


def solution(mesh):
    fine = Mesh(mesh.devices.reshape(4, 8, 4, 2), EVERYONE)
    mpo = ("y", "core")
    return jax.shard_map(
        on_device,
        mesh=fine,
        in_specs=(
            P(SECTOR, None, None),
            P(SECTOR, None, None),
            P(SECTOR),
            P(SECTOR),
            P(mpo, SECTOR, None, None),
            P(mpo, SECTOR, None, None),
            P(mpo),
            P(mpo),
        ),
        out_specs=(P(SECTOR, mpo, None), P()),
        check_vma=False,
    )
```

```python
import functools

import jax
import jax.numpy as jnp
from jax import lax
from jax.experimental import pallas as pl
from jax.experimental.pallas import tpu as pltpu
from jax.sharding import Mesh
from jax.sharding import PartitionSpec as P

ITERS = 4
BLOCK = 256
HALF = BLOCK // 2
SHARE = 32
SHARES = HALF // SHARE
SPINS = 2
CELLS = 3 * SPINS
SUMS = 6
SECTOR = ("x", "z")
EVERYONE = ("x", "z", "y", "core")
BF16 = jnp.bfloat16
F32 = jnp.float32
TURN = F32
VMEM_LIMIT = 24 * 1024 * 1024

HALF_BLOCK = (SPINS, HALF, BLOCK)
SIDE = (CELLS, HALF, BLOCK)


def block_rows_of(share, core):
    return pl.ds(pl.multiple_of((2 * share + core) * SHARE, SHARE), SHARE)


def half_rows_of(share):
    return pl.ds(pl.multiple_of(share * SHARE, SHARE), SHARE)


def inside_of(rows, cols, spin, first_row, count):
    row = lax.broadcasted_iota(jnp.int32, (count, BLOCK), 0) + first_row
    col = lax.broadcasted_iota(jnp.int32, (count, BLOCK), 1)
    return (row < rows[spin]) & (col < cols[spin])


def pair_sum(product):
    total = product[:8]
    for start in range(8, product.shape[0], 8):
        total = total + product[start : start + 8]
    return total[:, :128] + total[:, 128:]


def pick(sums, index):
    lane = lax.broadcasted_iota(jnp.int32, sums.shape, 1)
    return jnp.sum(jnp.where(lane == index, sums, 0.0), axis=1, keepdims=True)


def reduced(totals):
    lane = lax.broadcasted_iota(jnp.int32, (1, 128), 1)
    row = jnp.zeros((1, 128), F32)
    for at, total in enumerate(totals):
        value = jnp.sum(jnp.sum(total, axis=0, keepdims=True), axis=1, keepdims=True)
        row = row + jnp.where(lane == at, value, 0.0)
    return row


def zeros(count):
    return tuple(jnp.zeros((8, 128), F32) for _ in range(count))


def guess_kernel(rows, cols, guess, vector, vector_b):
    core = lax.axis_index("core")
    for spin in range(SPINS):
        for share in range(SHARES):
            there = block_rows_of(share, core)
            here = half_rows_of(share)
            inside = inside_of(rows, cols, spin, (2 * share + core) * SHARE, SHARE)
            value = jnp.where(inside, guess[spin, there, :], 0.0)
            vector[spin, here, :] = value
            vector_b[spin, here, :] = value.astype(BF16)


def diagonal_kernel(rows, cols, diagonal, vector, diag, inverse, sums):
    core = lax.axis_index("core")
    totals = zeros(SUMS)
    for spin in range(SPINS):
        for share in range(SHARES):
            here = half_rows_of(share)
            inside = inside_of(rows, cols, spin, (2 * share + core) * SHARE, SHARE)
            d = diagonal[spin, block_rows_of(share, core), :]
            diag[spin, here, :] = d
            inverse[spin, here, :] = jnp.where(inside, 1.0 / d, 0.0)
            value = vector[spin, here, :]
            totals = totals[:1] + (totals[1] + pair_sum(value * value),) + totals[2:5] + (
                totals[5] + pair_sum(value * value * d),
            )
    sums[...] = jnp.broadcast_to(reduced(totals), sums.shape)


def gather_halves(vector_b, slots):
    core = lax.axis_index("core")
    for slot, own, other in slots:
        for piece, half in ((own, core), (other, 1 - core)):
            for spin in range(SPINS):
                for share in range(SHARES):
                    vector_b[slot * SPINS + spin, block_rows_of(share, half), :] = piece[
                        spin, half_rows_of(share), :
                    ]


def cell_of(shifts, indices, w, spin):
    charges = lax.axis_size("x") * lax.axis_size("z")
    own_charge = lax.axis_index("x") * lax.axis_size("z") + lax.axis_index("z")
    charge = shifts[w]
    there = own_charge - charge
    source = spin - shifts[indices + w]
    on_grid = (source >= 0) & (source < SPINS) & (there >= 0) & (there < charges)
    return jnp.where(on_grid, (1 - charge) * SPINS + source, CELLS)


def turned_kernel(shifts, own, other, left, right, total, vector_b):
    indices = left.shape[0]
    gather_halves(vector_b, ((0, own, other),))
    total[...] = jnp.zeros_like(total)
    for spin in range(SPINS):
        for w in range(indices):
            back = lax.dot_general(
                left[w, spin], vector_b[spin], (((0,), (0,)), ((), ())),
                preferred_element_type=F32,
            ).astype(BF16)
            total[cell_of(shifts, indices, w, spin)] += jnp.dot(
                back, right[w, spin], preferred_element_type=F32
            )


def forward_kernel(
    last, copies, shifts, zero_a, low_a, high_a, zero_b, low_b, high_b, left, right, state_sums,
    *rest
):
    if last:
        sums, vector_b, ahead = rest
    else:
        turned, keep, send, sums, vector_b, ahead = rest
    core = lax.axis_index("core")
    indices = left.shape[0]
    gather_halves(
        vector_b, ((0, low_a, low_b), (1, zero_a, zero_b), (2, high_a, high_b))
    )
    vector_b[CELLS] = jnp.zeros((BLOCK, BLOCK), BF16)
    for spin in range(SPINS):
        for w in range(indices):
            cell = cell_of(shifts, indices, w, spin)
            middle = jnp.dot(
                left[w, spin], vector_b[cell], preferred_element_type=F32
            ).astype(BF16)
            term = lax.dot_general(
                middle, right[w, spin], (((1,), (1,)), ((), ())), preferred_element_type=F32
            )
            if w == 0:
                ahead[spin] = term
            else:
                ahead[spin] += term
    energy = jnp.zeros((8, 128), F32)
    for spin in range(SPINS):

        def one(index, energy, spin=spin):
            there = pl.ds(pl.multiple_of(index * SHARE, SHARE), SHARE)
            vector = vector_b[SPINS + spin, there, :].astype(F32)
            return energy + pair_sum(ahead[spin, there, :] * vector)

        energy = lax.fori_loop(0, BLOCK // SHARE, one, energy, unroll=True)
    row = reduced(zeros(SUMS - 1) + (2.0 * energy,)) + state_sums[0:1, :] * (1.0 / copies)
    sums[...] = jnp.broadcast_to(row, sums.shape)
    if last:
        return
    for cell in range(CELLS):
        for share in range(SHARES):
            here = half_rows_of(share)
            mine = turned[cell, block_rows_of(share, core), :]
            others = turned[cell, block_rows_of(share, 1 - core), :]
            if cell // SPINS == 1:
                mine = mine + ahead[cell - SPINS, block_rows_of(share, core), :]
                others = others + ahead[cell - SPINS, block_rows_of(share, 1 - core), :]
            keep[cell, here, :] = mine
            send[cell, here, :] = others.astype(BF16)


def image_rows(spin, here, part, turn_one, turn_two, turn_three):
    return (part[spin, here, :].astype(F32) + turn_two[spin, here, :].astype(F32)) + (
        turn_one[spin, here, :].astype(F32) + turn_three[spin, here, :].astype(F32)
    )


def rotation(t, rayleigh):
    corr = t(0)
    image_p = t(3) + rayleigh * corr
    image_x = t(4) + rayleigh * t(2)
    length_sq = jnp.maximum(t(1) - corr * corr * (2.0 - t(2)), 0.0)
    inv_length = lax.rsqrt(length_sq + 1e-06)
    off_diag = (image_p - corr * image_x) * inv_length
    corr_energy = (t(5) - 2.0 * corr * image_p + corr * corr * image_x) * inv_length * inv_length
    half_gap = 0.5 * (corr_energy - rayleigh)
    lowest = 0.5 * (rayleigh + corr_energy) - jnp.sqrt(half_gap * half_gap + off_diag * off_diag)
    weight_old = corr_energy - lowest
    length_pair = jnp.sqrt(weight_old * weight_old + off_diag * off_diag)
    mix = -off_diag / length_pair * inv_length
    return weight_old / length_pair - mix * corr, mix, lowest


def step_kernel(first, norm, gathered, part, turn_one, turn_two, turn_three, *rest):
    if first:
        (diag, inverse, p_in, x_out, res_out, p_out, p_b, ray_out, sums_out) = rest
    else:
        (diag, inverse, x_in, res_in, p_in, ray_in,
         x_out, res_out, p_out, p_b, ray_out, sums_out) = rest
    sums = jnp.sum(gathered[...], axis=0, keepdims=True) * (1.0 / norm)

    def t(at):
        return pick(sums, at)

    if first:
        m = lax.rsqrt(t(1) + 1e-06)
        new = t(5) * m * m
        shift = -new
    else:
        old = ray_in[0:1, 0:1]
        a, m, new = rotation(t, old)
        shift = old - new
    ray_out[...] = jnp.broadcast_to(new, ray_out.shape)
    step = 16

    def one(spin, index, totals):
        here = pl.ds(pl.multiple_of(index * step, step), step)
        summed = image_rows(spin, here, part, turn_one, turn_two, turn_three)
        d = diag[spin, here, :]
        p = p_in[spin, here, :]
        image = summed + d * p
        if first:
            x = m * p
            res = m * image + shift * x
        else:
            x = a * x_in[spin, here, :] + m * p
            res = a * res_in[spin, here, :] + m * (image - old * p) + shift * x
        new_p = res * inverse[spin, here, :]
        x_out[spin, here, :] = x
        res_out[spin, here, :] = res
        p_out[spin, here, :] = new_p
        p_b[spin, here, :] = new_p.astype(BF16)
        pairs = ((x, new_p), (new_p, new_p), (x, x), (res, new_p), (res, x), (new_p * d, new_p))
        return tuple(total + pair_sum(u * v) for total, (u, v) in zip(totals, pairs))

    totals = zeros(SUMS)
    for spin in range(SPINS):
        totals = lax.fori_loop(0, HALF // step, functools.partial(one, spin), totals)
    sums_out[...] = jnp.broadcast_to(reduced(totals), sums_out.shape)


def end_kernel(norm, gathered, ray_in, x_in, p_in, out, energy):
    sums = jnp.sum(gathered[...], axis=0, keepdims=True) * (1.0 / norm)
    a, m, new = rotation(lambda at: pick(sums, at), ray_in[0:1, 0:1])
    here = half_rows_of(lax.axis_index("y"))
    for spin in range(SPINS):
        out[spin] = a * x_in[spin, here, :] + m * p_in[spin, here, :]
    energy[0, 0] = new[0, 0]


def shape(dims, dtype):
    return jax.ShapeDtypeStruct(dims, dtype)


def call(kernel, scalars, arrays, outs, scratch=(), out_specs=None, cost=None):
    vmem = pl.BlockSpec(memory_space=pltpu.VMEM)
    return pl.pallas_call(
        kernel,
        in_specs=[pl.BlockSpec(memory_space=pltpu.SMEM)] * len(scalars) + [vmem] * len(arrays),
        out_specs=out_specs or [vmem] * len(outs),
        out_shape=outs,
        scratch_shapes=scratch,
        cost_estimate=cost,
        compiler_params=pltpu.CompilerParams(vmem_limit_bytes=VMEM_LIMIT),
    )(*scalars, *arrays)


def on_device(
    guess, diagonal, block_rows, block_cols, left_env, right_env, charge_shift, spin_shift
):
    sectors = lax.axis_size("x") * lax.axis_size("z")
    y_size = lax.axis_size("y")
    peers = sectors * lax.axis_size("core")
    everyone = peers * y_size
    norm = float(sectors * SPINS * BLOCK * BLOCK)
    upward = [(i, (i + 1) % sectors) for i in range(sectors)]
    downward = [(j, i) for i, j in upward]
    core_pair = [(0, 1), (1, 0)]
    shifts = jnp.concatenate([charge_shift, spin_shift])

    def other_core(value):
        return lax.ppermute(value, "core", core_pair)

    def products(p_b, state_sums, last):
        low_a = lax.ppermute(p_b, SECTOR, upward)
        high_a = lax.ppermute(p_b, SECTOR, downward)
        zero_b = other_core(p_b)
        pieces = [p_b, low_a, high_a, zero_b, other_core(low_a), other_core(high_a)]
        envs = [left_env, right_env]
        outs = [shape((everyone, 128), F32)]
        extra = []
        if not last:
            outs = [shape(SIDE, F32), shape(SIDE, BF16)] + outs
            extra = call(
                turned_kernel, [shifts], [p_b, zero_b, *envs],
                [shape((CELLS + 1, BLOCK, BLOCK), F32)],
                [pltpu.VMEM((SPINS, BLOCK, BLOCK), BF16)],
                cost=pl.CostEstimate(
                    flops=40 * BLOCK**3, bytes_accessed=5 * 2**20, transcendentals=0
                ),
            )
        return call(
            functools.partial(forward_kernel, last, y_size), [shifts],
            [*pieces, *envs, state_sums, *extra], outs,
            [
                pltpu.VMEM((CELLS + 1, BLOCK, BLOCK), BF16),
                pltpu.VMEM((SPINS, BLOCK, BLOCK), F32),
            ],
        )

    def gather(sums):
        return lax.all_to_all(sums, EVERYONE, 0, 0, tiled=True)

    def image_parts(keep, send, sums):
        both = keep + other_core(send).astype(F32)
        from_high = lax.ppermute(both[:SPINS].astype(BF16), SECTOR, downward)
        from_low = lax.ppermute(both[2 * SPINS :].astype(BF16), SECTOR, upward)
        part = both[SPINS : 2 * SPINS] + from_high.astype(F32) + from_low.astype(F32)
        part, sums = lax.optimization_barrier((part.astype(TURN), sums))
        turns = [
            lax.ppermute(part, "y", [(i, (i + turn) % y_size) for i in range(y_size)])
            for turn in (1, 2, 3)
        ]
        return [gather(sums), part, *turns]

    state = shape(HALF_BLOCK, F32)
    state_b = shape(HALF_BLOCK, BF16)
    flat = shape((8, 128), F32)
    masks = [block_rows, block_cols]
    p, p_b = call(guess_kernel, masks, [guess], [state, state_b])
    diag, inverse, state_sums = call(
        diagonal_kernel, masks, [diagonal, p], [state, state, flat]
    )
    before = [p]
    for iteration in range(ITERS):
        parts = image_parts(*products(p_b, state_sums, False))
        vector, residual, p, p_b, rayleigh, state_sums = call(
            functools.partial(step_kernel, iteration == 0, norm), [],
            [*parts, diag, inverse, *before],
            [state] * 3 + [state_b, flat, flat],
        )
        before = [vector, residual, p, rayleigh]
    gathered = gather(products(p_b, state_sums, True)[0])
    vmem = pl.BlockSpec(memory_space=pltpu.VMEM)
    ground_state, energy = call(
        functools.partial(end_kernel, norm), [], [gathered, rayleigh, vector, p],
        [shape((SPINS, SHARE, BLOCK), F32), shape((1, 1), F32)],
        out_specs=[vmem, pl.BlockSpec(memory_space=pltpu.SMEM)],
    )
    return ground_state, energy[0, 0]


def solution(mesh):
    fine = Mesh(mesh.devices.reshape(4, 8, 4, 2), EVERYONE)
    mpo = ("y", "core")
    return jax.shard_map(
        on_device,
        mesh=fine,
        in_specs=(
            P(SECTOR, None, None),
            P(SECTOR, None, None),
            P(SECTOR),
            P(SECTOR),
            P(mpo, SECTOR, None, None),
            P(mpo, SECTOR, None, None),
            P(mpo),
            P(mpo),
        ),
        out_specs=(P(SECTOR, mpo, None), P()),
        check_vma=False,
    )
```

```python
import functools

import jax
import jax.numpy as jnp
from jax import lax
from jax.experimental import pallas as pl
from jax.experimental.pallas import tpu as pltpu
from jax.sharding import Mesh
from jax.sharding import PartitionSpec as P

ITERS = 4
BLOCK = 256
HALF = BLOCK // 2
SHARE = 32
SHARES = HALF // SHARE
SPINS = 2
CELLS = 3 * SPINS
SUMS = 6
SECTOR = ("x", "z")
MPO = ("y", "core")
EVERYONE = SECTOR + MPO
BF16 = jnp.bfloat16
F32 = jnp.float32
TURN = F32
VMEM_LIMIT = 24 * 1024 * 1024

HALF_BLOCK = (SPINS, HALF, BLOCK)
SIDE = (CELLS, HALF, BLOCK)


def block_rows_of(share, core):
    return pl.ds(pl.multiple_of((2 * share + core) * SHARE, SHARE), SHARE)


def half_rows_of(share):
    return pl.ds(pl.multiple_of(share * SHARE, SHARE), SHARE)


def inside_of(rows, cols, spin, first_row, count):
    row = lax.broadcasted_iota(jnp.int32, (count, BLOCK), 0) + first_row
    col = lax.broadcasted_iota(jnp.int32, (count, BLOCK), 1)
    return (row < rows[spin]) & (col < cols[spin])


def pair_sum(product):
    total = product[:8]
    for start in range(8, product.shape[0], 8):
        total = total + product[start : start + 8]
    return total[:, :128] + total[:, 128:]


def pick(sums, index):
    lane = lax.broadcasted_iota(jnp.int32, sums.shape, 1)
    return jnp.sum(jnp.where(lane == index, sums, 0.0), axis=1, keepdims=True)


def reduced(totals):
    lane = lax.broadcasted_iota(jnp.int32, (1, 128), 1)
    row = jnp.zeros((1, 128), F32)
    for at, total in enumerate(totals):
        value = jnp.sum(jnp.sum(total, axis=0, keepdims=True), axis=1, keepdims=True)
        row = row + jnp.where(lane == at, value, 0.0)
    return row


def zeros(count):
    return tuple(jnp.zeros((8, 128), F32) for _ in range(count))


def guess_kernel(rows, cols, guess, vector, vector_b):
    core = lax.axis_index("core")
    for spin in range(SPINS):
        for share in range(SHARES):
            there = block_rows_of(share, core)
            here = half_rows_of(share)
            inside = inside_of(rows, cols, spin, (2 * share + core) * SHARE, SHARE)
            value = jnp.where(inside, guess[spin, there, :], 0.0)
            vector[spin, here, :] = value
            vector_b[spin, here, :] = value.astype(BF16)


def diagonal_kernel(rows, cols, diagonal, vector, diag, inverse, sums):
    core = lax.axis_index("core")
    totals = zeros(SUMS)
    for spin in range(SPINS):
        for share in range(SHARES):
            here = half_rows_of(share)
            inside = inside_of(rows, cols, spin, (2 * share + core) * SHARE, SHARE)
            d = diagonal[spin, block_rows_of(share, core), :]
            diag[spin, here, :] = d
            inverse[spin, here, :] = jnp.where(inside, 1.0 / d, 0.0)
            value = vector[spin, here, :]
            totals = totals[:1] + (totals[1] + pair_sum(value * value),) + totals[2:5] + (
                totals[5] + pair_sum(value * value * d),
            )
    sums[...] = jnp.broadcast_to(reduced(totals), sums.shape)


def gather_halves(vector_b, slots):
    core = lax.axis_index("core")
    for slot, own, other in slots:
        for piece, half in ((own, core), (other, 1 - core)):
            for spin in range(SPINS):
                for share in range(SHARES):
                    vector_b[slot * SPINS + spin, block_rows_of(share, half), :] = piece[
                        spin, half_rows_of(share), :
                    ]


def cell_of(shifts, indices, w, spin):
    charges = lax.axis_size("x") * lax.axis_size("z")
    own_charge = lax.axis_index("x") * lax.axis_size("z") + lax.axis_index("z")
    charge = shifts[w]
    there = own_charge - charge
    source = spin - shifts[indices + w]
    on_grid = (source >= 0) & (source < SPINS) & (there >= 0) & (there < charges)
    return jnp.where(on_grid, (1 - charge) * SPINS + source, CELLS)


def turned_kernel(shifts, own, other, left, right, total, vector_b):
    indices = left.shape[0]
    gather_halves(vector_b, ((0, own, other),))
    total[...] = jnp.zeros_like(total)
    for spin in range(SPINS):
        for w in range(indices):
            back = lax.dot_general(
                left[w, spin], vector_b[spin], (((0,), (0,)), ((), ())),
                preferred_element_type=F32,
            ).astype(BF16)
            total[cell_of(shifts, indices, w, spin)] += jnp.dot(
                back, right[w, spin], preferred_element_type=F32
            )


def forward_kernel(
    last, copies, shifts, zero_a, low_a, high_a, zero_b, low_b, high_b, left, right, state_sums,
    *rest
):
    if last:
        sums, vector_b, ahead = rest
    else:
        turned, keep, send, sums, vector_b, ahead = rest
    core = lax.axis_index("core")
    indices = left.shape[0]
    gather_halves(
        vector_b, ((0, low_a, low_b), (1, zero_a, zero_b), (2, high_a, high_b))
    )
    vector_b[CELLS] = jnp.zeros((BLOCK, BLOCK), BF16)
    for spin in range(SPINS):
        for w in range(indices):
            cell = cell_of(shifts, indices, w, spin)
            middle = jnp.dot(
                left[w, spin], vector_b[cell], preferred_element_type=F32
            ).astype(BF16)
            term = lax.dot_general(
                middle, right[w, spin], (((1,), (1,)), ((), ())), preferred_element_type=F32
            )
            if w == 0:
                ahead[spin] = term
            else:
                ahead[spin] += term
    energy = jnp.zeros((8, 128), F32)
    for spin in range(SPINS):

        def one(index, energy, spin=spin):
            there = pl.ds(pl.multiple_of(index * SHARE, SHARE), SHARE)
            vector = vector_b[SPINS + spin, there, :].astype(F32)
            return energy + pair_sum(ahead[spin, there, :] * vector)

        energy = lax.fori_loop(0, BLOCK // SHARE, one, energy, unroll=True)
    row = reduced(zeros(SUMS - 1) + (2.0 * energy,)) + state_sums[0:1, :] * (1.0 / copies)
    sums[...] = jnp.broadcast_to(row, sums.shape)
    if last:
        return
    for cell in range(CELLS):
        for share in range(SHARES):
            here = half_rows_of(share)
            mine = turned[cell, block_rows_of(share, core), :]
            others = turned[cell, block_rows_of(share, 1 - core), :]
            if cell // SPINS == 1:
                mine = mine + ahead[cell - SPINS, block_rows_of(share, core), :]
                others = others + ahead[cell - SPINS, block_rows_of(share, 1 - core), :]
            keep[cell, here, :] = mine
            send[cell, here, :] = others.astype(BF16)


def image_rows(spin, here, part, turn_one, turn_two, turn_three):
    return (part[spin, here, :].astype(F32) + turn_two[spin, here, :].astype(F32)) + (
        turn_one[spin, here, :].astype(F32) + turn_three[spin, here, :].astype(F32)
    )


def relay_kernel(gathered, sums):
    sums[...] = jnp.broadcast_to(jnp.sum(gathered[...], axis=0, keepdims=True), sums.shape)


def rotation(t, rayleigh):
    corr = t(0)
    image_p = t(3) + rayleigh * corr
    image_x = t(4) + rayleigh * t(2)
    length_sq = jnp.maximum(t(1) - corr * corr * (2.0 - t(2)), 0.0)
    inv_length = lax.rsqrt(length_sq + 1e-06)
    off_diag = (image_p - corr * image_x) * inv_length
    corr_energy = (t(5) - 2.0 * corr * image_p + corr * corr * image_x) * inv_length * inv_length
    half_gap = 0.5 * (corr_energy - rayleigh)
    lowest = 0.5 * (rayleigh + corr_energy) - jnp.sqrt(half_gap * half_gap + off_diag * off_diag)
    weight_old = corr_energy - lowest
    length_pair = jnp.sqrt(weight_old * weight_old + off_diag * off_diag)
    mix = -off_diag / length_pair * inv_length
    return weight_old / length_pair - mix * corr, mix, lowest


def step_kernel(first, norm, gathered, part, turn_one, turn_two, turn_three, *rest):
    if first:
        (diag, inverse, p_in, x_out, res_out, p_out, p_b, ray_out, sums_out) = rest
    else:
        (diag, inverse, x_in, res_in, p_in, ray_in,
         x_out, res_out, p_out, p_b, ray_out, sums_out) = rest
    sums = jnp.sum(gathered[...], axis=0, keepdims=True) * (1.0 / norm)

    def t(at):
        return pick(sums, at)

    if first:
        m = lax.rsqrt(t(1) + 1e-06)
        new = t(5) * m * m
        shift = -new
    else:
        old = ray_in[0:1, 0:1]
        a, m, new = rotation(t, old)
        shift = old - new
    ray_out[...] = jnp.broadcast_to(new, ray_out.shape)
    step = 16

    def one(spin, index, totals):
        here = pl.ds(pl.multiple_of(index * step, step), step)
        summed = image_rows(spin, here, part, turn_one, turn_two, turn_three)
        d = diag[spin, here, :]
        p = p_in[spin, here, :]
        image = summed + d * p
        if first:
            x = m * p
            res = m * image + shift * x
        else:
            x = a * x_in[spin, here, :] + m * p
            res = a * res_in[spin, here, :] + m * (image - old * p) + shift * x
        new_p = res * inverse[spin, here, :]
        x_out[spin, here, :] = x
        res_out[spin, here, :] = res
        p_out[spin, here, :] = new_p
        p_b[spin, here, :] = new_p.astype(BF16)
        pairs = ((x, new_p), (new_p, new_p), (x, x), (res, new_p), (res, x), (new_p * d, new_p))
        return tuple(total + pair_sum(u * v) for total, (u, v) in zip(totals, pairs))

    totals = zeros(SUMS)
    for spin in range(SPINS):
        totals = lax.fori_loop(0, HALF // step, functools.partial(one, spin), totals)
    sums_out[...] = jnp.broadcast_to(reduced(totals), sums_out.shape)


def end_kernel(norm, gathered, ray_in, x_in, p_in, out, energy):
    sums = jnp.sum(gathered[...], axis=0, keepdims=True) * (1.0 / norm)
    a, m, new = rotation(lambda at: pick(sums, at), ray_in[0:1, 0:1])
    here = half_rows_of(lax.axis_index("y"))
    for spin in range(SPINS):
        out[spin] = a * x_in[spin, here, :] + m * p_in[spin, here, :]
    energy[0, 0] = new[0, 0]


def shape(dims, dtype):
    return jax.ShapeDtypeStruct(dims, dtype)


def call(kernel, scalars, arrays, outs, scratch=(), out_specs=None, cost=None):
    vmem = pl.BlockSpec(memory_space=pltpu.VMEM)
    return pl.pallas_call(
        kernel,
        in_specs=[pl.BlockSpec(memory_space=pltpu.SMEM)] * len(scalars) + [vmem] * len(arrays),
        out_specs=out_specs or [vmem] * len(outs),
        out_shape=outs,
        scratch_shapes=scratch,
        cost_estimate=cost,
        compiler_params=pltpu.CompilerParams(vmem_limit_bytes=VMEM_LIMIT),
    )(*scalars, *arrays)


def on_device(
    guess, diagonal, block_rows, block_cols, left_env, right_env, charge_shift, spin_shift
):
    sectors = lax.axis_size("x") * lax.axis_size("z")
    y_size = lax.axis_size("y")
    mpo = y_size * lax.axis_size("core")
    everyone = sectors * mpo
    norm = float(sectors * SPINS * BLOCK * BLOCK)
    upward = [(i, (i + 1) % sectors) for i in range(sectors)]
    downward = [(j, i) for i, j in upward]
    core_pair = [(0, 1), (1, 0)]
    shifts = jnp.concatenate([charge_shift, spin_shift])

    def other_core(value):
        return lax.ppermute(value, "core", core_pair)

    def products(p_b, state_sums, last):
        low_a = lax.ppermute(p_b, SECTOR, upward)
        high_a = lax.ppermute(p_b, SECTOR, downward)
        zero_b = other_core(p_b)
        pieces = [p_b, low_a, high_a, zero_b, other_core(low_a), other_core(high_a)]
        envs = [left_env, right_env]
        outs = [shape((everyone if last else mpo, 128), F32)]
        extra = []
        if not last:
            outs = [shape(SIDE, F32), shape(SIDE, BF16)] + outs
            extra = call(
                turned_kernel, [shifts], [p_b, zero_b, *envs],
                [shape((CELLS + 1, BLOCK, BLOCK), F32)],
                [pltpu.VMEM((SPINS, BLOCK, BLOCK), BF16)],
                cost=pl.CostEstimate(
                    flops=40 * BLOCK**3, bytes_accessed=5 * 2**20, transcendentals=0
                ),
            )
        return call(
            functools.partial(forward_kernel, last, y_size), [shifts],
            [*pieces, *envs, state_sums, *extra], outs,
            [
                pltpu.VMEM((CELLS + 1, BLOCK, BLOCK), BF16),
                pltpu.VMEM((SPINS, BLOCK, BLOCK), F32),
            ],
        )

    def gather(sums, axes):
        return lax.all_to_all(sums, axes, 0, 0, tiled=True)

    def image_parts(keep, send, sums):
        both = keep + other_core(send).astype(F32)
        to_low, to_high, sums = lax.optimization_barrier(
            (both[:SPINS].astype(BF16), both[2 * SPINS :].astype(BF16), sums)
        )
        from_high = lax.ppermute(to_low, SECTOR, downward)
        from_low = lax.ppermute(to_high, SECTOR, upward)
        sums = call(relay_kernel, [], [gather(sums, MPO)], [shape((sectors, 128), F32)])[0]
        part = both[SPINS : 2 * SPINS] + from_high.astype(F32) + from_low.astype(F32)
        part, sums = lax.optimization_barrier((part.astype(TURN), sums))
        turns = [
            lax.ppermute(part, "y", [(i, (i + turn) % y_size) for i in range(y_size)])
            for turn in (1, 2, 3)
        ]
        return [gather(sums, SECTOR), part, *turns]

    state = shape(HALF_BLOCK, F32)
    state_b = shape(HALF_BLOCK, BF16)
    flat = shape((8, 128), F32)
    masks = [block_rows, block_cols]
    p, p_b = call(guess_kernel, masks, [guess], [state, state_b])
    diag, inverse, state_sums = call(
        diagonal_kernel, masks, [diagonal, p], [state, state, flat]
    )
    before = [p]
    for iteration in range(ITERS):
        parts = image_parts(*products(p_b, state_sums, False))
        vector, residual, p, p_b, rayleigh, state_sums = call(
            functools.partial(step_kernel, iteration == 0, norm), [],
            [*parts, diag, inverse, *before],
            [state] * 3 + [state_b, flat, flat],
        )
        before = [vector, residual, p, rayleigh]
    gathered = gather(products(p_b, state_sums, True)[0], EVERYONE)
    vmem = pl.BlockSpec(memory_space=pltpu.VMEM)
    ground_state, energy = call(
        functools.partial(end_kernel, norm), [], [gathered, rayleigh, vector, p],
        [shape((SPINS, SHARE, BLOCK), F32), shape((1, 1), F32)],
        out_specs=[vmem, pl.BlockSpec(memory_space=pltpu.SMEM)],
    )
    return ground_state, energy[0, 0]


def solution(mesh):
    fine = Mesh(mesh.devices.reshape(4, 8, 4, 2), EVERYONE)
    return jax.shard_map(
        on_device,
        mesh=fine,
        in_specs=(
            P(SECTOR, None, None),
            P(SECTOR, None, None),
            P(SECTOR),
            P(SECTOR),
            P(MPO, SECTOR, None, None),
            P(MPO, SECTOR, None, None),
            P(MPO),
            P(MPO),
        ),
        out_specs=(P(SECTOR, MPO, None), P()),
        check_vma=False,
    )
```

```python
import functools

import jax
import jax.numpy as jnp
from jax import lax
from jax.experimental import pallas as pl
from jax.experimental.pallas import tpu as pltpu
from jax.sharding import Mesh
from jax.sharding import PartitionSpec as P

ITERS = 4
BLOCK = 256
HALF = BLOCK // 2
SHARE = 32
SHARES = HALF // SHARE
SPINS = 2
CELLS = 3 * SPINS
SUMS = 6
SECTOR = ("x", "z")
MPO = ("y", "core")
EVERYONE = SECTOR + MPO
BF16 = jnp.bfloat16
F32 = jnp.float32
TURN = F32
VMEM_LIMIT = 24 * 1024 * 1024

HALF_BLOCK = (SPINS, HALF, BLOCK)
SIDE = (CELLS, HALF, BLOCK)


def block_rows_of(share, core):
    return pl.ds(pl.multiple_of((2 * share + core) * SHARE, SHARE), SHARE)


def half_rows_of(share):
    return pl.ds(pl.multiple_of(share * SHARE, SHARE), SHARE)


def inside_of(rows, cols, spin, first_row, count):
    row = lax.broadcasted_iota(jnp.int32, (count, BLOCK), 0) + first_row
    col = lax.broadcasted_iota(jnp.int32, (count, BLOCK), 1)
    return (row < rows[spin]) & (col < cols[spin])


def pair_sum(product):
    total = product[:8]
    for start in range(8, product.shape[0], 8):
        total = total + product[start : start + 8]
    return total[:, :128] + total[:, 128:]


def pick(sums, index):
    lane = lax.broadcasted_iota(jnp.int32, sums.shape, 1)
    return jnp.sum(jnp.where(lane == index, sums, 0.0), axis=1, keepdims=True)


def reduced(totals):
    lane = lax.broadcasted_iota(jnp.int32, (1, 128), 1)
    row = jnp.zeros((1, 128), F32)
    for at, total in enumerate(totals):
        value = jnp.sum(jnp.sum(total, axis=0, keepdims=True), axis=1, keepdims=True)
        row = row + jnp.where(lane == at, value, 0.0)
    return row


def zeros(count):
    return tuple(jnp.zeros((8, 128), F32) for _ in range(count))


def guess_kernel(rows, cols, guess, vector, vector_b):
    core = lax.axis_index("core")
    for spin in range(SPINS):
        for share in range(SHARES):
            there = block_rows_of(share, core)
            here = half_rows_of(share)
            inside = inside_of(rows, cols, spin, (2 * share + core) * SHARE, SHARE)
            value = jnp.where(inside, guess[spin, there, :], 0.0)
            vector[spin, here, :] = value
            vector_b[spin, here, :] = value.astype(BF16)


def diagonal_kernel(rows, cols, diagonal, vector, diag, inverse, sums):
    core = lax.axis_index("core")
    totals = zeros(SUMS)
    for spin in range(SPINS):
        for share in range(SHARES):
            here = half_rows_of(share)
            inside = inside_of(rows, cols, spin, (2 * share + core) * SHARE, SHARE)
            d = diagonal[spin, block_rows_of(share, core), :]
            diag[spin, here, :] = d
            inverse[spin, here, :] = jnp.where(inside, 1.0 / d, 0.0)
            value = vector[spin, here, :]
            totals = totals[:1] + (totals[1] + pair_sum(value * value),) + totals[2:5] + (
                totals[5] + pair_sum(value * value * d),
            )
    sums[...] = jnp.broadcast_to(reduced(totals), sums.shape)


def gather_halves(vector_b, slots):
    core = lax.axis_index("core")
    for slot, own, other in slots:
        for piece, half in ((own, core), (other, 1 - core)):
            for spin in range(SPINS):
                for share in range(SHARES):
                    vector_b[slot * SPINS + spin, block_rows_of(share, half), :] = piece[
                        spin, half_rows_of(share), :
                    ]


def cell_of(shifts, indices, w, spin):
    charges = lax.axis_size("x") * lax.axis_size("z")
    own_charge = lax.axis_index("x") * lax.axis_size("z") + lax.axis_index("z")
    charge = shifts[w]
    there = own_charge - charge
    source = spin - shifts[indices + w]
    on_grid = (source >= 0) & (source < SPINS) & (there >= 0) & (there < charges)
    return jnp.where(on_grid, (1 - charge) * SPINS + source, CELLS)


def turned_kernel(shifts, own, other, left, right, total, vector_b):
    indices = left.shape[0]
    gather_halves(vector_b, ((0, own, other),))
    total[...] = jnp.zeros_like(total)
    for spin in range(SPINS):
        for w in range(indices):
            back = lax.dot_general(
                left[w, spin], vector_b[spin], (((0,), (0,)), ((), ())),
                preferred_element_type=F32,
            ).astype(BF16)
            total[cell_of(shifts, indices, w, spin)] += jnp.dot(
                back, right[w, spin], preferred_element_type=F32
            )


def forward_kernel(
    last, copies, shifts, zero_a, low_a, high_a, zero_b, low_b, high_b, left, right, state_sums,
    *rest
):
    if last:
        sums, vector_b, ahead = rest
    else:
        turned, keep, send, sums, vector_b, ahead = rest
    core = lax.axis_index("core")
    indices = left.shape[0]
    gather_halves(
        vector_b, ((0, low_a, low_b), (1, zero_a, zero_b), (2, high_a, high_b))
    )
    vector_b[CELLS] = jnp.zeros((BLOCK, BLOCK), BF16)
    for spin in range(SPINS):
        for w in range(indices):
            cell = cell_of(shifts, indices, w, spin)
            middle = jnp.dot(
                left[w, spin], vector_b[cell], preferred_element_type=F32
            ).astype(BF16)
            term = lax.dot_general(
                middle, right[w, spin], (((1,), (1,)), ((), ())), preferred_element_type=F32
            )
            if w == 0:
                ahead[spin] = term
            else:
                ahead[spin] += term
    energy = jnp.zeros((8, 128), F32)
    for spin in range(SPINS):

        def one(index, energy, spin=spin):
            there = pl.ds(pl.multiple_of(index * SHARE, SHARE), SHARE)
            vector = vector_b[SPINS + spin, there, :].astype(F32)
            return energy + pair_sum(ahead[spin, there, :] * vector)

        energy = lax.fori_loop(0, BLOCK // SHARE, one, energy, unroll=True)
    row = reduced(zeros(SUMS - 1) + (2.0 * energy,)) + state_sums[0:1, :] * (1.0 / copies)
    sums[...] = jnp.broadcast_to(row, sums.shape)
    if last:
        return
    for cell in range(CELLS):
        for share in range(SHARES):
            here = half_rows_of(share)
            mine = turned[cell, block_rows_of(share, core), :]
            others = turned[cell, block_rows_of(share, 1 - core), :]
            if cell // SPINS == 1:
                mine = mine + ahead[cell - SPINS, block_rows_of(share, core), :]
                others = others + ahead[cell - SPINS, block_rows_of(share, 1 - core), :]
            keep[cell, here, :] = mine
            send[cell, here, :] = others.astype(BF16)


def image_rows(spin, here, part, turn_one, turn_two, turn_three):
    return (part[spin, here, :].astype(F32) + turn_two[spin, here, :].astype(F32)) + (
        turn_one[spin, here, :].astype(F32) + turn_three[spin, here, :].astype(F32)
    )


def relay_kernel(gathered, sums):
    sums[...] = jnp.broadcast_to(jnp.sum(gathered[...], axis=0, keepdims=True), sums.shape)


def rotation(t, rayleigh):
    corr = t(0)
    image_p = t(3) + rayleigh * corr
    image_x = t(4) + rayleigh * t(2)
    length_sq = jnp.maximum(t(1) - corr * corr * (2.0 - t(2)), 0.0)
    inv_length = lax.rsqrt(length_sq + 1e-06)
    off_diag = (image_p - corr * image_x) * inv_length
    corr_energy = (t(5) - 2.0 * corr * image_p + corr * corr * image_x) * inv_length * inv_length
    half_gap = 0.5 * (corr_energy - rayleigh)
    lowest = 0.5 * (rayleigh + corr_energy) - jnp.sqrt(half_gap * half_gap + off_diag * off_diag)
    weight_old = corr_energy - lowest
    length_pair = jnp.sqrt(weight_old * weight_old + off_diag * off_diag)
    mix = -off_diag / length_pair * inv_length
    return weight_old / length_pair - mix * corr, mix, lowest


def step_kernel(first, norm, gathered, part, turn_one, turn_two, turn_three, *rest):
    if first:
        (diag, inverse, p_in, x_out, res_out, p_out, p_b, ray_out, sums_out) = rest
    else:
        (diag, inverse, x_in, res_in, p_in, ray_in,
         x_out, res_out, p_out, p_b, ray_out, sums_out) = rest
    sums = jnp.sum(gathered[...], axis=0, keepdims=True) * (1.0 / norm)

    def t(at):
        return pick(sums, at)

    if first:
        m = lax.rsqrt(t(1) + 1e-06)
        new = t(5) * m * m
        shift = -new
    else:
        old = ray_in[0:1, 0:1]
        a, m, new = rotation(t, old)
        shift = old - new
    ray_out[...] = jnp.broadcast_to(new, ray_out.shape)
    step = 16

    def one(spin, index, totals):
        here = pl.ds(pl.multiple_of(index * step, step), step)
        summed = image_rows(spin, here, part, turn_one, turn_two, turn_three)
        d = diag[spin, here, :]
        p = p_in[spin, here, :]
        image = summed + d * p
        if first:
            x = m * p
            res = m * image + shift * x
        else:
            x = a * x_in[spin, here, :] + m * p
            res = a * res_in[spin, here, :] + m * (image - old * p) + shift * x
        new_p = res * inverse[spin, here, :]
        x_out[spin, here, :] = x
        res_out[spin, here, :] = res
        p_out[spin, here, :] = new_p
        p_b[spin, here, :] = new_p.astype(BF16)
        pairs = ((x, new_p), (new_p, new_p), (x, x), (res, new_p), (res, x), (new_p * d, new_p))
        return tuple(total + pair_sum(u * v) for total, (u, v) in zip(totals, pairs))

    totals = zeros(SUMS)
    for spin in range(SPINS):
        totals = lax.fori_loop(0, HALF // step, functools.partial(one, spin), totals)
    sums_out[...] = jnp.broadcast_to(reduced(totals), sums_out.shape)


def end_kernel(norm, gathered, ray_in, x_in, p_in, out, energy):
    sums = jnp.sum(gathered[...], axis=0, keepdims=True) * (1.0 / norm)
    a, m, new = rotation(lambda at: pick(sums, at), ray_in[0:1, 0:1])
    here = half_rows_of(lax.axis_index("y"))
    for spin in range(SPINS):
        out[spin] = a * x_in[spin, here, :] + m * p_in[spin, here, :]
    energy[0, 0] = new[0, 0]


def shape(dims, dtype):
    return jax.ShapeDtypeStruct(dims, dtype)


def call(kernel, scalars, arrays, outs, scratch=(), out_specs=None, cost=None):
    vmem = pl.BlockSpec(memory_space=pltpu.VMEM)
    return pl.pallas_call(
        kernel,
        in_specs=[pl.BlockSpec(memory_space=pltpu.SMEM)] * len(scalars) + [vmem] * len(arrays),
        out_specs=out_specs or [vmem] * len(outs),
        out_shape=outs,
        scratch_shapes=scratch,
        cost_estimate=cost,
        compiler_params=pltpu.CompilerParams(vmem_limit_bytes=VMEM_LIMIT),
    )(*scalars, *arrays)


def on_device(
    guess, diagonal, block_rows, block_cols, left_env, right_env, charge_shift, spin_shift
):
    sectors = lax.axis_size("x") * lax.axis_size("z")
    y_size = lax.axis_size("y")
    mpo = y_size * lax.axis_size("core")
    everyone = sectors * mpo
    norm = float(sectors * SPINS * BLOCK * BLOCK)
    upward = [(i, (i + 1) % sectors) for i in range(sectors)]
    downward = [(j, i) for i, j in upward]
    core_pair = [(0, 1), (1, 0)]
    shifts = jnp.concatenate([charge_shift, spin_shift])

    def other_core(value):
        return lax.ppermute(value, "core", core_pair)

    def products(p_b, state_sums, last):
        low_a = lax.ppermute(p_b, SECTOR, upward)
        high_a = lax.ppermute(p_b, SECTOR, downward)
        zero_b = other_core(p_b)
        pieces = [p_b, low_a, high_a, zero_b, other_core(low_a), other_core(high_a)]
        envs = [left_env, right_env]
        outs = [shape((everyone if last else mpo, 128), F32)]
        extra = []
        if not last:
            outs = [shape(SIDE, F32), shape(SIDE, BF16)] + outs
            extra = call(
                turned_kernel, [shifts], [p_b, zero_b, *envs],
                [shape((CELLS + 1, BLOCK, BLOCK), F32)],
                [pltpu.VMEM((SPINS, BLOCK, BLOCK), BF16)],
                cost=pl.CostEstimate(
                    flops=40 * BLOCK**3, bytes_accessed=5 * 2**20, transcendentals=0
                ),
            )
        return call(
            functools.partial(forward_kernel, last, y_size), [shifts],
            [*pieces, *envs, state_sums, *extra], outs,
            [
                pltpu.VMEM((CELLS + 1, BLOCK, BLOCK), BF16),
                pltpu.VMEM((SPINS, BLOCK, BLOCK), F32),
            ],
        )

    def gather(sums, axes):
        return lax.all_to_all(sums, axes, 0, 0, tiled=True)

    def image_parts(keep, send, sums):
        both = keep + other_core(send).astype(F32)
        to_low, to_high, sums = lax.optimization_barrier(
            (both[:SPINS].astype(BF16), both[2 * SPINS :].astype(BF16), sums)
        )
        from_high = lax.ppermute(to_low, SECTOR, downward)
        from_low = lax.ppermute(to_high, SECTOR, upward)
        sums = call(relay_kernel, [], [gather(sums, MPO)], [shape((sectors, 128), F32)])[0]
        part = both[SPINS : 2 * SPINS] + from_high.astype(F32) + from_low.astype(F32)
        part, sums = lax.optimization_barrier((part.astype(TURN), sums))
        turns = [
            lax.ppermute(part, "y", [(i, i ^ turn) for i in range(y_size)])
            for turn in (1, 2, 3)
        ]
        return [gather(sums, SECTOR), part, *turns]

    state = shape(HALF_BLOCK, F32)
    state_b = shape(HALF_BLOCK, BF16)
    flat = shape((8, 128), F32)
    masks = [block_rows, block_cols]
    p, p_b = call(guess_kernel, masks, [guess], [state, state_b])
    diag, inverse, state_sums = call(
        diagonal_kernel, masks, [diagonal, p], [state, state, flat]
    )
    before = [p]
    for iteration in range(ITERS):
        parts = image_parts(*products(p_b, state_sums, False))
        vector, residual, p, p_b, rayleigh, state_sums = call(
            functools.partial(step_kernel, iteration == 0, norm), [],
            [*parts, diag, inverse, *before],
            [state] * 3 + [state_b, flat, flat],
        )
        before = [vector, residual, p, rayleigh]
    gathered = gather(products(p_b, state_sums, True)[0], EVERYONE)
    vmem = pl.BlockSpec(memory_space=pltpu.VMEM)
    ground_state, energy = call(
        functools.partial(end_kernel, norm), [], [gathered, rayleigh, vector, p],
        [shape((SPINS, SHARE, BLOCK), F32), shape((1, 1), F32)],
        out_specs=[vmem, pl.BlockSpec(memory_space=pltpu.SMEM)],
    )
    return ground_state, energy[0, 0]


def solution(mesh):
    fine = Mesh(mesh.devices.reshape(4, 8, 4, 2), EVERYONE)
    return jax.shard_map(
        on_device,
        mesh=fine,
        in_specs=(
            P(SECTOR, None, None),
            P(SECTOR, None, None),
            P(SECTOR),
            P(SECTOR),
            P(MPO, SECTOR, None, None),
            P(MPO, SECTOR, None, None),
            P(MPO),
            P(MPO),
        ),
        out_specs=(P(SECTOR, MPO, None), P()),
        check_vma=False,
    )
```

```python
import functools

import jax
import jax.numpy as jnp
from jax import lax
from jax.experimental import pallas as pl
from jax.experimental.pallas import tpu as pltpu
from jax.sharding import Mesh
from jax.sharding import PartitionSpec as P

ITERS = 4
BLOCK = 256
HALF = BLOCK // 2
SHARE = 32
SHARES = HALF // SHARE
SPINS = 2
CELLS = 3 * SPINS
SUMS = 6
SECTOR = ("x", "z")
MPO = ("y", "core")
EVERYONE = SECTOR + MPO
BF16 = jnp.bfloat16
F32 = jnp.float32
TURN = F32
VMEM_LIMIT = 24 * 1024 * 1024

HALF_BLOCK = (SPINS, HALF, BLOCK)
SIDE = (CELLS, HALF, BLOCK)


def block_rows_of(share, core):
    return pl.ds(pl.multiple_of((2 * share + core) * SHARE, SHARE), SHARE)


def half_rows_of(share):
    return pl.ds(pl.multiple_of(share * SHARE, SHARE), SHARE)


def inside_of(info, spin, first_row, count):
    row = lax.broadcasted_iota(jnp.int32, (count, BLOCK), 0) + first_row
    col = lax.broadcasted_iota(jnp.int32, (count, BLOCK), 1)
    return (row < info[spin]) & (col < info[SPINS + spin])


def pair_sum(product):
    total = product[:8]
    for start in range(8, product.shape[0], 8):
        total = total + product[start : start + 8]
    return total[:, :128] + total[:, 128:]


def pick(sums, index):
    lane = lax.broadcasted_iota(jnp.int32, sums.shape, 1)
    return jnp.sum(jnp.where(lane == index, sums, 0.0), axis=1, keepdims=True)


def reduced(totals):
    lane = lax.broadcasted_iota(jnp.int32, (1, 128), 1)
    row = jnp.zeros((1, 128), F32)
    for at, total in enumerate(totals):
        value = jnp.sum(jnp.sum(total, axis=0, keepdims=True), axis=1, keepdims=True)
        row = row + jnp.where(lane == at, value, 0.0)
    return row


def zeros(count):
    return tuple(jnp.zeros((8, 128), F32) for _ in range(count))


def guess_kernel(info, guess, vector, vector_b):
    core = lax.axis_index("core")
    for spin in range(SPINS):
        for share in range(SHARES):
            there = block_rows_of(share, core)
            here = half_rows_of(share)
            inside = inside_of(info, spin, (2 * share + core) * SHARE, SHARE)
            value = jnp.where(inside, guess[spin, there, :], 0.0)
            vector[spin, here, :] = value
            vector_b[spin, here, :] = value.astype(BF16)


def diagonal_kernel(info, diagonal, vector, diag, inverse, sums):
    core = lax.axis_index("core")
    totals = zeros(SUMS)
    for spin in range(SPINS):
        for share in range(SHARES):
            here = half_rows_of(share)
            inside = inside_of(info, spin, (2 * share + core) * SHARE, SHARE)
            d = diagonal[spin, block_rows_of(share, core), :]
            diag[spin, here, :] = d
            inverse[spin, here, :] = jnp.where(inside, 1.0 / d, 0.0)
            value = vector[spin, here, :]
            totals = totals[:1] + (totals[1] + pair_sum(value * value),) + totals[2:5] + (
                totals[5] + pair_sum(value * value * d),
            )
    sums[...] = jnp.broadcast_to(reduced(totals), sums.shape)


def gather_halves(vector_b, slots):
    core = lax.axis_index("core")
    for slot, own, other in slots:
        for piece, half in ((own, core), (other, 1 - core)):
            for spin in range(SPINS):
                for share in range(SHARES):
                    vector_b[slot * SPINS + spin, block_rows_of(share, half), :] = piece[
                        spin, half_rows_of(share), :
                    ]


def cell_of(info, indices, w, spin):
    charges = lax.axis_size("x") * lax.axis_size("z")
    own_charge = lax.axis_index("x") * lax.axis_size("z") + lax.axis_index("z")
    charge = info[2 * SPINS + w]
    there = own_charge - charge
    source = spin - info[2 * SPINS + indices + w]
    on_grid = (source >= 0) & (source < SPINS) & (there >= 0) & (there < charges)
    return jnp.where(on_grid, (1 - charge) * SPINS + source, CELLS)


def turned_kernel(info, own, other, left, right, total, vector_b):
    indices = left.shape[0]
    gather_halves(vector_b, ((0, own, other),))
    total[...] = jnp.zeros_like(total)
    for spin in range(SPINS):
        for w in range(indices):
            back = lax.dot_general(
                left[w, spin], vector_b[spin], (((0,), (0,)), ((), ())),
                preferred_element_type=F32,
            ).astype(BF16)
            total[cell_of(info, indices, w, spin)] += jnp.dot(
                back, right[w, spin], preferred_element_type=F32
            )


def forward_kernel(
    last, copies, info, zero_a, low_a, high_a, zero_b, low_b, high_b, left, right, state_sums,
    *rest
):
    if last:
        sums, vector_b, ahead = rest
    else:
        turned, keep, send, sums, vector_b, ahead = rest
    core = lax.axis_index("core")
    indices = left.shape[0]
    gather_halves(
        vector_b, ((0, low_a, low_b), (1, zero_a, zero_b), (2, high_a, high_b))
    )
    vector_b[CELLS] = jnp.zeros((BLOCK, BLOCK), BF16)
    for spin in range(SPINS):
        for w in range(indices):
            cell = cell_of(info, indices, w, spin)
            middle = jnp.dot(
                left[w, spin], vector_b[cell], preferred_element_type=F32
            ).astype(BF16)
            term = lax.dot_general(
                middle, right[w, spin], (((1,), (1,)), ((), ())), preferred_element_type=F32
            )
            if w == 0:
                ahead[spin] = term
            else:
                ahead[spin] += term
    energy = jnp.zeros((8, 128), F32)
    for spin in range(SPINS):

        def one(index, energy, spin=spin):
            there = pl.ds(pl.multiple_of(index * SHARE, SHARE), SHARE)
            vector = vector_b[SPINS + spin, there, :].astype(F32)
            return energy + pair_sum(ahead[spin, there, :] * vector)

        energy = lax.fori_loop(0, BLOCK // SHARE, one, energy, unroll=True)
    row = reduced(zeros(SUMS - 1) + (2.0 * energy,)) + state_sums[0:1, :] * (1.0 / copies)
    sums[...] = jnp.broadcast_to(row, sums.shape)
    if last:
        return
    for cell in range(CELLS):
        for share in range(SHARES):
            here = half_rows_of(share)
            mine = turned[cell, block_rows_of(share, core), :]
            others = turned[cell, block_rows_of(share, 1 - core), :]
            if cell // SPINS == 1:
                mine = mine + ahead[cell - SPINS, block_rows_of(share, core), :]
                others = others + ahead[cell - SPINS, block_rows_of(share, 1 - core), :]
            keep[cell, here, :] = mine
            send[cell, here, :] = others.astype(BF16)


def image_rows(spin, here, part, turn_one, turn_two, turn_three):
    return (part[spin, here, :].astype(F32) + turn_two[spin, here, :].astype(F32)) + (
        turn_one[spin, here, :].astype(F32) + turn_three[spin, here, :].astype(F32)
    )


def relay_kernel(gathered, sums):
    sums[...] = jnp.broadcast_to(jnp.sum(gathered[...], axis=0, keepdims=True), sums.shape)


def rotation(t, rayleigh):
    corr = t(0)
    image_p = t(3) + rayleigh * corr
    image_x = t(4) + rayleigh * t(2)
    length_sq = jnp.maximum(t(1) - corr * corr * (2.0 - t(2)), 0.0)
    inv_length = lax.rsqrt(length_sq + 1e-06)
    off_diag = (image_p - corr * image_x) * inv_length
    corr_energy = (t(5) - 2.0 * corr * image_p + corr * corr * image_x) * inv_length * inv_length
    half_gap = 0.5 * (corr_energy - rayleigh)
    lowest = 0.5 * (rayleigh + corr_energy) - jnp.sqrt(half_gap * half_gap + off_diag * off_diag)
    weight_old = corr_energy - lowest
    length_pair = jnp.sqrt(weight_old * weight_old + off_diag * off_diag)
    mix = -off_diag / length_pair * inv_length
    return weight_old / length_pair - mix * corr, mix, lowest


def step_kernel(first, norm, gathered, part, turn_one, turn_two, turn_three, *rest):
    if first:
        (diag, inverse, p_in, x_out, res_out, p_out, p_b, ray_out, sums_out) = rest
    else:
        (diag, inverse, x_in, res_in, p_in, ray_in,
         x_out, res_out, p_out, p_b, ray_out, sums_out) = rest
    sums = jnp.sum(gathered[...], axis=0, keepdims=True) * (1.0 / norm)

    def t(at):
        return pick(sums, at)

    if first:
        m = lax.rsqrt(t(1) + 1e-06)
        new = t(5) * m * m
        shift = -new
    else:
        old = ray_in[0:1, 0:1]
        a, m, new = rotation(t, old)
        shift = old - new
    ray_out[...] = jnp.broadcast_to(new, ray_out.shape)
    step = 16

    def one(spin, index, totals):
        here = pl.ds(pl.multiple_of(index * step, step), step)
        summed = image_rows(spin, here, part, turn_one, turn_two, turn_three)
        d = diag[spin, here, :]
        p = p_in[spin, here, :]
        image = summed + d * p
        if first:
            x = m * p
            res = m * image + shift * x
        else:
            x = a * x_in[spin, here, :] + m * p
            res = a * res_in[spin, here, :] + m * (image - old * p) + shift * x
        new_p = res * inverse[spin, here, :]
        x_out[spin, here, :] = x
        res_out[spin, here, :] = res
        p_out[spin, here, :] = new_p
        p_b[spin, here, :] = new_p.astype(BF16)
        pairs = ((x, new_p), (new_p, new_p), (x, x), (res, new_p), (res, x), (new_p * d, new_p))
        return tuple(total + pair_sum(u * v) for total, (u, v) in zip(totals, pairs))

    totals = zeros(SUMS)
    for spin in range(SPINS):
        totals = lax.fori_loop(0, HALF // step, functools.partial(one, spin), totals)
    sums_out[...] = jnp.broadcast_to(reduced(totals), sums_out.shape)


def end_kernel(norm, gathered, ray_in, x_in, p_in, out, energy):
    sums = jnp.sum(gathered[...], axis=0, keepdims=True) * (1.0 / norm)
    a, m, new = rotation(lambda at: pick(sums, at), ray_in[0:1, 0:1])
    here = half_rows_of(lax.axis_index("y"))
    for spin in range(SPINS):
        out[spin] = a * x_in[spin, here, :] + m * p_in[spin, here, :]
    energy[0, 0] = new[0, 0]


def shape(dims, dtype):
    return jax.ShapeDtypeStruct(dims, dtype)


def call(kernel, scalars, arrays, outs, scratch=(), out_specs=None, cost=None):
    vmem = pl.BlockSpec(memory_space=pltpu.VMEM)
    return pl.pallas_call(
        kernel,
        in_specs=[pl.BlockSpec(memory_space=pltpu.SMEM)] * len(scalars) + [vmem] * len(arrays),
        out_specs=out_specs or [vmem] * len(outs),
        out_shape=outs,
        scratch_shapes=scratch,
        cost_estimate=cost,
        compiler_params=pltpu.CompilerParams(vmem_limit_bytes=VMEM_LIMIT),
    )(*scalars, *arrays)


def on_device(
    guess, diagonal, block_rows, block_cols, left_env, right_env, charge_shift, spin_shift
):
    sectors = lax.axis_size("x") * lax.axis_size("z")
    y_size = lax.axis_size("y")
    mpo = y_size * lax.axis_size("core")
    everyone = sectors * mpo
    norm = float(sectors * SPINS * BLOCK * BLOCK)
    upward = [(i, (i + 1) % sectors) for i in range(sectors)]
    downward = [(j, i) for i, j in upward]
    core_pair = [(0, 1), (1, 0)]
    info = jnp.concatenate([block_rows, block_cols, charge_shift, spin_shift])

    def other_core(value):
        return lax.ppermute(value, "core", core_pair)

    def products(p_b, state_sums, first, last):
        low_a = lax.ppermute(p_b, SECTOR, upward)
        high_a = lax.ppermute(p_b, SECTOR, downward)
        zero_b = other_core(p_b)
        envs = [left_env, right_env]
        outs = [shape((everyone if last else mpo, 128), F32)]
        extra = []
        if not last:
            outs = [shape(SIDE, F32), shape(SIDE, BF16)] + outs
            extra = call(
                turned_kernel, [info], [p_b, zero_b, *envs],
                [shape((CELLS + 1, BLOCK, BLOCK), F32)],
                [pltpu.VMEM((SPINS, BLOCK, BLOCK), BF16)],
                cost=pl.CostEstimate(
                    flops=40 * BLOCK**3, bytes_accessed=5 * 2**20, transcendentals=0
                ),
            )
            if first:
                low_a, high_a, *extra = lax.optimization_barrier((low_a, high_a, *extra))
        pieces = [p_b, low_a, high_a, zero_b, other_core(low_a), other_core(high_a)]
        return call(
            functools.partial(forward_kernel, last, y_size), [info],
            [*pieces, *envs, state_sums, *extra], outs,
            [
                pltpu.VMEM((CELLS + 1, BLOCK, BLOCK), BF16),
                pltpu.VMEM((SPINS, BLOCK, BLOCK), F32),
            ],
        )

    def gather(sums, axes):
        return lax.all_to_all(sums, axes, 0, 0, tiled=True)

    def image_parts(keep, send, sums):
        both = keep + other_core(send).astype(F32)
        to_low, to_high, sums = lax.optimization_barrier(
            (both[:SPINS].astype(BF16), both[2 * SPINS :].astype(BF16), sums)
        )
        from_high = lax.ppermute(to_low, SECTOR, downward)
        from_low = lax.ppermute(to_high, SECTOR, upward)
        sums = call(relay_kernel, [], [gather(sums, MPO)], [shape((sectors, 128), F32)])[0]
        part = both[SPINS : 2 * SPINS] + from_high.astype(F32) + from_low.astype(F32)
        part, sums = lax.optimization_barrier((part.astype(TURN), sums))
        turns = [
            lax.ppermute(part, "y", [(i, i ^ turn) for i in range(y_size)])
            for turn in (1, 2, 3)
        ]
        return [gather(sums, SECTOR), part, *turns]

    state = shape(HALF_BLOCK, F32)
    state_b = shape(HALF_BLOCK, BF16)
    flat = shape((8, 128), F32)
    p, p_b = call(guess_kernel, [info], [guess], [state, state_b])
    diag, inverse, state_sums = call(
        diagonal_kernel, [info], [diagonal, p], [state, state, flat]
    )
    before = [p]
    for iteration in range(ITERS):
        parts = image_parts(*products(p_b, state_sums, iteration == 0, False))
        vector, residual, p, p_b, rayleigh, state_sums = call(
            functools.partial(step_kernel, iteration == 0, norm), [],
            [*parts, diag, inverse, *before],
            [state] * 3 + [state_b, flat, flat],
        )
        before = [vector, residual, p, rayleigh]
    gathered = gather(products(p_b, state_sums, False, True)[0], EVERYONE)
    vmem = pl.BlockSpec(memory_space=pltpu.VMEM)
    ground_state, energy = call(
        functools.partial(end_kernel, norm), [], [gathered, rayleigh, vector, p],
        [shape((SPINS, SHARE, BLOCK), F32), shape((1, 1), F32)],
        out_specs=[vmem, pl.BlockSpec(memory_space=pltpu.SMEM)],
    )
    return ground_state, energy[0, 0]


def solution(mesh):
    fine = Mesh(mesh.devices.reshape(4, 8, 4, 2), EVERYONE)
    return jax.shard_map(
        on_device,
        mesh=fine,
        in_specs=(
            P(SECTOR, None, None),
            P(SECTOR, None, None),
            P(SECTOR),
            P(SECTOR),
            P(MPO, SECTOR, None, None),
            P(MPO, SECTOR, None, None),
            P(MPO),
            P(MPO),
        ),
        out_specs=(P(SECTOR, MPO, None), P()),
        check_vma=False,
    )
```

```python
import functools

import jax
import jax.numpy as jnp
from jax import lax
from jax.experimental import pallas as pl
from jax.experimental.pallas import tpu as pltpu
from jax.sharding import Mesh
from jax.sharding import PartitionSpec as P

ITERS = 4
BLOCK = 256
HALF = BLOCK // 2
SHARE = 32
SHARES = HALF // SHARE
SPINS = 2
CELLS = 3 * SPINS
SUMS = 6
SECTOR = ("x", "z")
MPO = ("y", "core")
EVERYONE = SECTOR + MPO
BF16 = jnp.bfloat16
F32 = jnp.float32
TURN = F32
VMEM_LIMIT = 24 * 1024 * 1024

HALF_BLOCK = (SPINS, HALF, BLOCK)
SIDE = (CELLS, HALF, BLOCK)


def block_rows_of(share, core):
    return pl.ds(pl.multiple_of((2 * share + core) * SHARE, SHARE), SHARE)


def half_rows_of(share):
    return pl.ds(pl.multiple_of(share * SHARE, SHARE), SHARE)


def inside_of(info, spin, first_row, count):
    row = lax.broadcasted_iota(jnp.int32, (count, BLOCK), 0) + first_row
    col = lax.broadcasted_iota(jnp.int32, (count, BLOCK), 1)
    return (row < info[spin]) & (col < info[SPINS + spin])


def pair_sum(product):
    total = product[:8]
    for start in range(8, product.shape[0], 8):
        total = total + product[start : start + 8]
    return total[:, :128] + total[:, 128:]


def pick(sums, index):
    lane = lax.broadcasted_iota(jnp.int32, sums.shape, 1)
    return jnp.sum(jnp.where(lane == index, sums, 0.0), axis=1, keepdims=True)


def reduced(totals):
    lane = lax.broadcasted_iota(jnp.int32, (1, 128), 1)
    row = jnp.zeros((1, 128), F32)
    for at, total in enumerate(totals):
        value = jnp.sum(jnp.sum(total, axis=0, keepdims=True), axis=1, keepdims=True)
        row = row + jnp.where(lane == at, value, 0.0)
    return row


def zeros(count):
    return tuple(jnp.zeros((8, 128), F32) for _ in range(count))


def guess_kernel(info, guess, vector, vector_b):
    core = lax.axis_index("core")
    for spin in range(SPINS):
        for share in range(SHARES):
            there = block_rows_of(share, core)
            here = half_rows_of(share)
            inside = inside_of(info, spin, (2 * share + core) * SHARE, SHARE)
            value = jnp.where(inside, guess[spin, there, :], 0.0)
            vector[spin, here, :] = value
            vector_b[spin, here, :] = value.astype(BF16)


def diagonal_kernel(info, diagonal, vector, diag, inverse, sums):
    core = lax.axis_index("core")
    totals = zeros(SUMS)
    for spin in range(SPINS):
        for share in range(SHARES):
            here = half_rows_of(share)
            inside = inside_of(info, spin, (2 * share + core) * SHARE, SHARE)
            d = diagonal[spin, block_rows_of(share, core), :]
            diag[spin, here, :] = d
            inverse[spin, here, :] = jnp.where(inside, 1.0 / d, 0.0)
            value = vector[spin, here, :]
            totals = totals[:1] + (totals[1] + pair_sum(value * value),) + totals[2:5] + (
                totals[5] + pair_sum(value * value * d),
            )
    sums[...] = jnp.broadcast_to(reduced(totals), sums.shape)


def gather_halves(vector_b, slots):
    core = lax.axis_index("core")
    for slot, own, other in slots:
        for piece, half in ((own, core), (other, 1 - core)):
            for spin in range(SPINS):
                for share in range(SHARES):
                    vector_b[slot * SPINS + spin, block_rows_of(share, half), :] = piece[
                        spin, half_rows_of(share), :
                    ]


def cell_of(info, indices, w, spin):
    charges = lax.axis_size("x") * lax.axis_size("z")
    own_charge = lax.axis_index("x") * lax.axis_size("z") + lax.axis_index("z")
    charge = info[2 * SPINS + w]
    there = own_charge - charge
    source = spin - info[2 * SPINS + indices + w]
    on_grid = (source >= 0) & (source < SPINS) & (there >= 0) & (there < charges)
    return jnp.where(on_grid, (1 - charge) * SPINS + source, CELLS)


def turned_kernel(info, own, other, left, right, total, vector_b):
    indices = left.shape[0]
    gather_halves(vector_b, ((0, own, other),))
    total[...] = jnp.zeros_like(total)
    for spin in range(SPINS):
        for w in range(indices):
            back = lax.dot_general(
                left[w, spin], vector_b[spin], (((0,), (0,)), ((), ())),
                preferred_element_type=F32,
            ).astype(BF16)
            total[cell_of(info, indices, w, spin)] += jnp.dot(
                back, right[w, spin], preferred_element_type=F32
            )


def forward_kernel(
    last, copies, info, zero_a, low_a, high_a, zero_b, low_b, high_b, left, right, state_sums,
    *rest
):
    if last:
        sums, vector_b, ahead = rest
    else:
        turned, keep, send, sums, vector_b, ahead = rest
    core = lax.axis_index("core")
    indices = left.shape[0]
    gather_halves(
        vector_b, ((0, low_a, low_b), (1, zero_a, zero_b), (2, high_a, high_b))
    )
    vector_b[CELLS] = jnp.zeros((BLOCK, BLOCK), BF16)
    for spin in range(SPINS):
        middles = [
            jnp.dot(
                left[w, spin], vector_b[cell_of(info, indices, w, spin)],
                preferred_element_type=F32,
            ).astype(BF16)
            for w in range(indices)
        ]
        ahead[spin] = lax.dot_general(
            jnp.concatenate(middles, axis=1),
            jnp.concatenate([right[w, spin] for w in range(indices)], axis=1),
            (((1,), (1,)), ((), ())), preferred_element_type=F32,
        )
    energy = jnp.zeros((8, 128), F32)
    for spin in range(SPINS):

        def one(index, energy, spin=spin):
            there = pl.ds(pl.multiple_of(index * SHARE, SHARE), SHARE)
            vector = vector_b[SPINS + spin, there, :].astype(F32)
            return energy + pair_sum(ahead[spin, there, :] * vector)

        energy = lax.fori_loop(0, BLOCK // SHARE, one, energy, unroll=True)
    row = reduced(zeros(SUMS - 1) + (2.0 * energy,)) + state_sums[0:1, :] * (1.0 / copies)
    sums[...] = jnp.broadcast_to(row, sums.shape)
    if last:
        return
    for cell in range(CELLS):
        for share in range(SHARES):
            here = half_rows_of(share)
            mine = turned[cell, block_rows_of(share, core), :]
            others = turned[cell, block_rows_of(share, 1 - core), :]
            if cell // SPINS == 1:
                mine = mine + ahead[cell - SPINS, block_rows_of(share, core), :]
                others = others + ahead[cell - SPINS, block_rows_of(share, 1 - core), :]
            keep[cell, here, :] = mine
            send[cell, here, :] = others.astype(BF16)


def image_rows(spin, here, part, turn_one, turn_two, turn_three):
    return (part[spin, here, :].astype(F32) + turn_two[spin, here, :].astype(F32)) + (
        turn_one[spin, here, :].astype(F32) + turn_three[spin, here, :].astype(F32)
    )


def relay_kernel(gathered, sums):
    sums[...] = jnp.broadcast_to(jnp.sum(gathered[...], axis=0, keepdims=True), sums.shape)


def rotation(t, rayleigh):
    corr = t(0)
    image_p = t(3) + rayleigh * corr
    image_x = t(4) + rayleigh * t(2)
    length_sq = jnp.maximum(t(1) - corr * corr * (2.0 - t(2)), 0.0)
    inv_length = lax.rsqrt(length_sq + 1e-06)
    off_diag = (image_p - corr * image_x) * inv_length
    corr_energy = (t(5) - 2.0 * corr * image_p + corr * corr * image_x) * inv_length * inv_length
    half_gap = 0.5 * (corr_energy - rayleigh)
    lowest = 0.5 * (rayleigh + corr_energy) - jnp.sqrt(half_gap * half_gap + off_diag * off_diag)
    weight_old = corr_energy - lowest
    length_pair = jnp.sqrt(weight_old * weight_old + off_diag * off_diag)
    mix = -off_diag / length_pair * inv_length
    return weight_old / length_pair - mix * corr, mix, lowest


def step_kernel(first, norm, gathered, part, turn_one, turn_two, turn_three, *rest):
    if first:
        (diag, inverse, p_in, x_out, res_out, p_out, p_b, ray_out, sums_out) = rest
    else:
        (diag, inverse, x_in, res_in, p_in, ray_in,
         x_out, res_out, p_out, p_b, ray_out, sums_out) = rest
    sums = jnp.sum(gathered[...], axis=0, keepdims=True) * (1.0 / norm)

    def t(at):
        return pick(sums, at)

    if first:
        m = lax.rsqrt(t(1) + 1e-06)
        new = t(5) * m * m
        shift = -new
    else:
        old = ray_in[0:1, 0:1]
        a, m, new = rotation(t, old)
        shift = old - new
    ray_out[...] = jnp.broadcast_to(new, ray_out.shape)
    step = 16

    def one(spin, index, totals):
        here = pl.ds(pl.multiple_of(index * step, step), step)
        summed = image_rows(spin, here, part, turn_one, turn_two, turn_three)
        d = diag[spin, here, :]
        p = p_in[spin, here, :]
        image = summed + d * p
        if first:
            x = m * p
            res = m * image + shift * x
        else:
            x = a * x_in[spin, here, :] + m * p
            res = a * res_in[spin, here, :] + m * (image - old * p) + shift * x
        new_p = res * inverse[spin, here, :]
        x_out[spin, here, :] = x
        res_out[spin, here, :] = res
        p_out[spin, here, :] = new_p
        p_b[spin, here, :] = new_p.astype(BF16)
        pairs = ((x, new_p), (new_p, new_p), (x, x), (res, new_p), (res, x), (new_p * d, new_p))
        return tuple(total + pair_sum(u * v) for total, (u, v) in zip(totals, pairs))

    totals = zeros(SUMS)
    for spin in range(SPINS):
        totals = lax.fori_loop(0, HALF // step, functools.partial(one, spin), totals)
    sums_out[...] = jnp.broadcast_to(reduced(totals), sums_out.shape)


def end_kernel(norm, gathered, ray_in, x_in, p_in, out, energy):
    sums = jnp.sum(gathered[...], axis=0, keepdims=True) * (1.0 / norm)
    a, m, new = rotation(lambda at: pick(sums, at), ray_in[0:1, 0:1])
    here = half_rows_of(lax.axis_index("y"))
    for spin in range(SPINS):
        out[spin] = a * x_in[spin, here, :] + m * p_in[spin, here, :]
    energy[0, 0] = new[0, 0]


def shape(dims, dtype):
    return jax.ShapeDtypeStruct(dims, dtype)


def call(kernel, scalars, arrays, outs, scratch=(), out_specs=None, cost=None):
    vmem = pl.BlockSpec(memory_space=pltpu.VMEM)
    return pl.pallas_call(
        kernel,
        in_specs=[pl.BlockSpec(memory_space=pltpu.SMEM)] * len(scalars) + [vmem] * len(arrays),
        out_specs=out_specs or [vmem] * len(outs),
        out_shape=outs,
        scratch_shapes=scratch,
        cost_estimate=cost,
        compiler_params=pltpu.CompilerParams(vmem_limit_bytes=VMEM_LIMIT),
    )(*scalars, *arrays)


def on_device(
    guess, diagonal, block_rows, block_cols, left_env, right_env, charge_shift, spin_shift
):
    sectors = lax.axis_size("x") * lax.axis_size("z")
    y_size = lax.axis_size("y")
    mpo = y_size * lax.axis_size("core")
    everyone = sectors * mpo
    norm = float(sectors * SPINS * BLOCK * BLOCK)
    upward = [(i, (i + 1) % sectors) for i in range(sectors)]
    downward = [(j, i) for i, j in upward]
    core_pair = [(0, 1), (1, 0)]
    info = jnp.concatenate([block_rows, block_cols, charge_shift, spin_shift])

    def other_core(value):
        return lax.ppermute(value, "core", core_pair)

    def products(p_b, state_sums, first, last):
        low_a = lax.ppermute(p_b, SECTOR, upward)
        high_a = lax.ppermute(p_b, SECTOR, downward)
        zero_b = other_core(p_b)
        envs = [left_env, right_env]
        outs = [shape((everyone if last else mpo, 128), F32)]
        extra = []
        if not last:
            outs = [shape(SIDE, F32), shape(SIDE, BF16)] + outs
            extra = call(
                turned_kernel, [info], [p_b, zero_b, *envs],
                [shape((CELLS + 1, BLOCK, BLOCK), F32)],
                [pltpu.VMEM((SPINS, BLOCK, BLOCK), BF16)],
                cost=pl.CostEstimate(
                    flops=40 * BLOCK**3, bytes_accessed=5 * 2**20, transcendentals=0
                ),
            )
            if first:
                low_a, high_a, *extra = lax.optimization_barrier((low_a, high_a, *extra))
        pieces = [p_b, low_a, high_a, zero_b, other_core(low_a), other_core(high_a)]
        return call(
            functools.partial(forward_kernel, last, y_size), [info],
            [*pieces, *envs, state_sums, *extra], outs,
            [
                pltpu.VMEM((CELLS + 1, BLOCK, BLOCK), BF16),
                pltpu.VMEM((SPINS, BLOCK, BLOCK), F32),
            ],
        )

    def gather(sums, axes):
        return lax.all_to_all(sums, axes, 0, 0, tiled=True)

    def image_parts(keep, send, sums):
        both = keep + other_core(send).astype(F32)
        to_low, to_high, sums = lax.optimization_barrier(
            (both[:SPINS].astype(BF16), both[2 * SPINS :].astype(BF16), sums)
        )
        from_high = lax.ppermute(to_low, SECTOR, downward)
        from_low = lax.ppermute(to_high, SECTOR, upward)
        sums = call(relay_kernel, [], [gather(sums, MPO)], [shape((sectors, 128), F32)])[0]
        part = both[SPINS : 2 * SPINS] + from_high.astype(F32) + from_low.astype(F32)
        part, sums = lax.optimization_barrier((part.astype(TURN), sums))
        turns = [
            lax.ppermute(part, "y", [(i, i ^ turn) for i in range(y_size)])
            for turn in (1, 2, 3)
        ]
        return [gather(sums, SECTOR), part, *turns]

    state = shape(HALF_BLOCK, F32)
    state_b = shape(HALF_BLOCK, BF16)
    flat = shape((8, 128), F32)
    p, p_b = call(guess_kernel, [info], [guess], [state, state_b])
    diag, inverse, state_sums = call(
        diagonal_kernel, [info], [diagonal, p], [state, state, flat]
    )
    before = [p]
    for iteration in range(ITERS):
        parts = image_parts(*products(p_b, state_sums, iteration == 0, False))
        vector, residual, p, p_b, rayleigh, state_sums = call(
            functools.partial(step_kernel, iteration == 0, norm), [],
            [*parts, diag, inverse, *before],
            [state] * 3 + [state_b, flat, flat],
        )
        before = [vector, residual, p, rayleigh]
    gathered = gather(products(p_b, state_sums, False, True)[0], EVERYONE)
    vmem = pl.BlockSpec(memory_space=pltpu.VMEM)
    ground_state, energy = call(
        functools.partial(end_kernel, norm), [], [gathered, rayleigh, vector, p],
        [shape((SPINS, SHARE, BLOCK), F32), shape((1, 1), F32)],
        out_specs=[vmem, pl.BlockSpec(memory_space=pltpu.SMEM)],
    )
    return ground_state, energy[0, 0]


def solution(mesh):
    fine = Mesh(mesh.devices.reshape(4, 8, 4, 2), EVERYONE)
    return jax.shard_map(
        on_device,
        mesh=fine,
        in_specs=(
            P(SECTOR, None, None),
            P(SECTOR, None, None),
            P(SECTOR),
            P(SECTOR),
            P(MPO, SECTOR, None, None),
            P(MPO, SECTOR, None, None),
            P(MPO),
            P(MPO),
        ),
        out_specs=(P(SECTOR, MPO, None), P()),
        check_vma=False,
    )
```
